32 devices in a mesh: dp: 8 (over y, x, core), tensor: 4 (over z).
Axes of the slice: x: 2, y: 2, z: 4, core: 2. Of those that a mesh axis runs over, the one named last changes fastest.
Arguments:
- tokens: bfloat16 [16384, 1152], P(('dp', 'tensor')), may hold values from -6 to 6
- conditioning: float32 [16, 1152], P('dp'), may hold values from -6 to 6
- master: float32 [4608, 72, 72], P(('dp', 'tensor')), may hold values from -1.06066017 to 1.06066017
- moment: float32 [4608, 72, 72], P(('dp', 'tensor')), may hold values from -384 to 384
- stats: float32 [2, 4608, 72, 72], P(None, ('dp', 'tensor')), may hold values from -187680.85 to 1179648, as said below
- roots: float32 [2, 4608, 72, 72], P(None, ('dp', 'tensor')), may hold values from -1 to 1
- cotangent: bfloat16 [16384, 1152], P(('dp', 'tensor')), may hold values from -6 to 6
Outputs:
- out_tokens: bfloat16 [16384, 1152], P(('dp', 'tensor'))
- grad_tokens: float32 [16384, 1152], P(('dp', 'tensor'))
- grad_conditioning: float32 [16, 1152], P('dp')
- new_master: float32 [4608, 72, 72], P(('dp', 'tensor'))
- new_moment: float32 [4608, 72, 72], P(('dp', 'tensor'))
- new_stats: float32 [2, 4608, 72, 72], P(None, ('dp', 'tensor'))
The draws below stay inside these ranges and needn't reach their ends.
Inputs may be any that keep to these rules, and one draw needn't show every extreme that they name: `stats`: each block of both statistics is symmetric.
All inputs are finite; a program needn't handle non-finite values.
Results may differ from the reference program's by a relative error of at most 0.015.
The reference program's roundings to bfloat16 on the way count: a program that leaves them out, or rounds other values in their place, can miss the bound.
Values may be sent and summed in bfloat16 or wider, within the bound.
No kernel may reach another device: no remote copies, remote signals or barrier semaphores. Data moves between devices by JAX's collectives and lax.ppermute only.
A program may use at most 256 MiB of HBM per device.

```python
import jax
import jax.numpy as jnp
from jax import lax

D = 1152
HEADS = 16
HEAD_DIM = 72
FF = 4608
B = 72
LEN = 1024
LATENTS = 16
TOKENS = 16384
QKV_DEV = 24
PROJ_DEV = 8
FC_DEV = 32
BLK_DEV = 144
NBLK = 4608
N_DP = 8
N_TENSOR = 4


def kind_levels(levels_table):
    local_index = jnp.arange(NBLK, dtype=jnp.int32) % BLK_DEV
    boundaries = [QKV_DEV, QKV_DEV + PROJ_DEV, QKV_DEV + PROJ_DEV + FC_DEV, QKV_DEV + PROJ_DEV + 2 * FC_DEV]
    block_scale = jnp.full((NBLK,), levels_table[4], jnp.float32)
    for boundary, level_here in reversed(list(zip(boundaries, levels_table[:4]))):
        block_scale = jnp.where(local_index < boundary, jnp.float32(level_here), block_scale)
    return block_scale


def grad_levels():
    root_tokens = TOKENS ** 0.5
    return kind_levels([0.5 * root_tokens, 0.1 * root_tokens, 0.5 * root_tokens, 0.5 * root_tokens, 0.4 * root_tokens])


def draw_master(key, part):
    block_scale = kind_levels([D ** (-0.5), 6.0 * D ** (-0.5), D ** (-0.5), FF ** (-0.5), D ** (-0.5)])
    noise = jnp.clip(jax.random.normal(key, (NBLK, B, B), jnp.float32), -6.0, 6.0)
    return noise * block_scale[:, None, None]


def draw_moment(key, part):
    noise = jnp.clip(jax.random.normal(key, (NBLK, B, B), jnp.float32), -6.0, 6.0)
    return noise * grad_levels()[:, None, None]


def draw_stats(key, part):
    squared = (grad_levels() ** 2)[None, :, None]
    diag_key = jax.random.fold_in(key, 11)
    off_key = jax.random.fold_in(key, 12)
    diagonal = B * squared * 4.0 ** jax.random.uniform(diag_key, (2, NBLK, B), jnp.float32)
    noise = jnp.clip(jax.random.normal(off_key, (2, NBLK, B, B), jnp.float32), -6.0, 6.0)
    noise = (noise + jnp.swapaxes(noise, -1, -2)) * (0.45 * B ** 0.5) * squared[..., None]
    identity = jnp.eye(B, dtype=jnp.float32)
    return noise * (1.0 - identity) + diagonal[..., None] * identity


def draw_roots(key, part):
    base_level = (2.0 * B * grad_levels() ** 2) ** (-0.25)
    base_level = base_level[None, :, None]
    diag_key = jax.random.fold_in(key, 21)
    off_key = jax.random.fold_in(key, 22)
    diagonal = base_level * 4.0 ** (jax.random.uniform(diag_key, (2, NBLK, B), jnp.float32) - 0.5)
    noise = jnp.clip(jax.random.normal(off_key, (2, NBLK, B, B), jnp.float32), -6.0, 6.0) * 0.06 * base_level[..., None]
    identity = jnp.eye(B, dtype=jnp.float32)
    return noise * (1.0 - identity) + diagonal[..., None] * identity


def steps_of(key, dims, split, low, largest):
    def one(axis_at, blocks):
        heights = jax.random.uniform(jax.random.fold_in(jax.random.fold_in(key, 6), axis_at), (blocks,), jnp.float32, low / len(split), largest / len(split))
        return jnp.repeat(jnp.exp(heights), dims[axis_at] // blocks).reshape((-1,) + (1,) * (len(dims) - axis_at - 1))

    loudness = one(*split[0])
    for cut in split[1:]:
        loudness = loudness * one(*cut)
    return loudness


def normal_values(key, extent, spread, limit, split=(), held_as=jnp.bfloat16):
    entries = spread * jax.random.normal(key, extent, jnp.float32)
    if split:
        entries = entries * steps_of(key, extent, split, -0.22, 0.18)
    return jnp.clip(entries, -limit, limit).astype(held_as)


def setup_inputs(seed: int = 0) -> dict:
    keys = jax.random.split(jax.random.key(seed), 8)
    return {
        "tokens": normal_values(keys[0], (TOKENS, D), 1.0, 6.0, ((0, 32),)),
        "conditioning": normal_values(keys[1], (LATENTS, D), 1.0, 6.0, ((0, 8),), jnp.float32),
        "master": draw_master(jax.random.fold_in(keys[7], 71), 0),
        "moment": draw_moment(jax.random.fold_in(keys[7], 71), 0),
        "stats": draw_stats(jax.random.fold_in(keys[7], 71), 0),
        "roots": draw_roots(jax.random.fold_in(keys[7], 71), 0),
        "cotangent": normal_values(keys[6], (TOKENS, D), 1.0, 6.0, ((0, 32),)),
    }


epsilon = 1e-06
momentum_decay = 0.9
learning_rate = 0.4
HIGHEST = lax.Precision.HIGHEST

@jax.custom_vjp
def low(v):
    return lax.optimization_barrier(v.astype(jnp.bfloat16)).astype(jnp.float32)

@jax.custom_vjp
def low_back(v):
    return v

def low_keep(v):
    return (low(v), None)

def low_pass(kept, grad):
    return (grad,)

def back_keep(v):
    return (v, None)

def back_low(kept, grad):
    return (low(grad),)
low.defvjp(low_keep, low_pass)
low_back.defvjp(back_keep, back_low)

def product(left_side, right_side):
    return jnp.dot(left_side, right_side, precision=HIGHEST, preferred_element_type=jnp.float32)

def layer_norm(values):
    center = values - lax.optimization_barrier(jnp.mean(values, axis=-1, keepdims=True))
    variance = lax.optimization_barrier(jnp.mean(center * center, axis=-1, keepdims=True))
    return center * lax.rsqrt(variance + epsilon)

def grid_shapes():
    row_blocks = D // B
    split_size = B * N_TENSOR
    return [(row_blocks, 3 * D // split_size), (D // split_size, row_blocks), (row_blocks, FF // split_size), (FF // split_size, row_blocks), (row_blocks, 6 * D // split_size)]

def to_matrices(flat):
    grouped = flat.reshape(N_DP, N_TENSOR, BLK_DEV, B, B)
    matrices = []
    offset = 0
    for row_blocks, col_blocks in grid_shapes():
        count_here = row_blocks * col_blocks // N_DP
        piece_blocks = jnp.transpose(grouped[:, :, offset:offset + count_here], (1, 0, 2, 3, 4))
        piece_blocks = piece_blocks.reshape(N_TENSOR, row_blocks, col_blocks, B, B)
        matrices.append(jnp.transpose(piece_blocks, (0, 1, 3, 2, 4)).reshape(N_TENSOR, row_blocks * B, col_blocks * B))
        offset += count_here
    return matrices

def full_weights(flat):
    w_qkv, w_out, w_up, w_down, w_ada = to_matrices(flat)
    heads_local = HEADS // N_TENSOR
    w_qkv = jnp.transpose(w_qkv.reshape(N_TENSOR, D, 3, heads_local, HEAD_DIM), (2, 1, 0, 3, 4)).reshape(3, D, D)
    w_out = w_out.reshape(D, D)
    w_up = jnp.transpose(w_up, (1, 0, 2)).reshape(D, FF)
    w_down = w_down.reshape(FF, D)
    w_ada = jnp.transpose(w_ada, (1, 0, 2)).reshape(D, 6 * D)
    return (w_qkv, w_out, w_up, w_down, w_ada)

def attend(pieces):
    query_rows, key_rows, value_rows = pieces
    factor = HEAD_DIM ** (-0.5)
    scores = low_back(jnp.einsum('qhd,khd->hqk', query_rows, key_rows, precision=HIGHEST) * factor)
    weights = low(jax.nn.softmax(scores, axis=-1))
    return jnp.einsum('hqk,khd->qhd', weights, value_rows, precision=HIGHEST)

def forward(tokens, conditioning, flat):
    w_qkv, w_out, w_up, w_down, w_ada = full_weights(low(flat))
    modulation = product(low(jax.nn.silu(conditioning)), w_ada).reshape(LATENTS, 6, 1, D)
    sequences = tokens.reshape(LATENTS, LEN, D)
    modulated_one = low(layer_norm(sequences) * (1.0 + modulation[:, 1]) + modulation[:, 0]).reshape(-1, D)
    projections = tuple((low(low_back(product(modulated_one, w_qkv[member]))).reshape(LATENTS, LEN, HEADS, HEAD_DIM) for member in range(3)))
    attended = lax.map(jax.checkpoint(attend), projections)
    attended = low(low_back(attended)).reshape(-1, D)
    branch = low_back(product(attended, w_out)).reshape(LATENTS, LEN, D)
    middle = sequences + modulation[:, 2] * branch
    modulated_two = low(layer_norm(middle) * (1.0 + modulation[:, 4]) + modulation[:, 3]).reshape(-1, D)
    pre_gelu = low_back(product(modulated_two, w_up))
    hidden = low(jax.nn.gelu(pre_gelu, approximate=True))
    feed_out = low_back(product(hidden, w_down)).reshape(LATENTS, LEN, D)
    return (middle + modulation[:, 5] * feed_out).reshape(-1, D)

def reference(tokens, conditioning, master, moment, stats, roots, cotangent):
    outputs, pullback = jax.vjp(forward, tokens.astype(jnp.float32), conditioning, master)
    grad_tokens, grad_conditioning, grad_blocks = pullback(cotangent.astype(jnp.float32))
    left_stats = 0.5 * stats[0] + 0.5 * jnp.einsum('nij,nkj->nik', grad_blocks, grad_blocks, precision=HIGHEST)
    right_stats = 0.5 * stats[1] + 0.5 * jnp.einsum('nji,njk->nik', grad_blocks, grad_blocks, precision=HIGHEST)
    new_moment = momentum_decay * moment + (1.0 - momentum_decay) * grad_blocks
    update = jnp.einsum('nij,njk->nik', roots[0], new_moment, precision=HIGHEST)
    update = jnp.einsum('nij,njk->nik', update, roots[1], precision=HIGHEST)
    new_master = master - learning_rate * update
    return (outputs.astype(jnp.bfloat16), grad_tokens, grad_conditioning, new_master, new_moment, jnp.stack([left_stats, right_stats]))
```

```python
from functools import partial
import math

import jax
import jax.numpy as jnp
from jax import lax
from jax.experimental import pallas as pl
from jax.experimental.pallas import tpu as pltpu
from jax.sharding import PartitionSpec as P

HEADS = 16
HEAD_DIM = 72
FF = 4608
LEN = 1024

epsilon = 1e-06
momentum_decay = 0.9
learning_rate = 0.4
HIGHEST = lax.Precision.HIGHEST
bf16 = jnp.bfloat16
f32 = jnp.float32
VMEM_LIMIT = 56 * 1024 * 1024


def layer_norm(values):
    center = values - jnp.mean(values, axis=-1, keepdims=True)
    variance = jnp.mean(center * center, axis=-1, keepdims=True)
    return center * lax.rsqrt(variance + epsilon)


def norm_back(values, gradient):
    center = values - jnp.mean(values, axis=-1, keepdims=True)
    variance = jnp.mean(center * center, axis=-1, keepdims=True)
    inverse = lax.rsqrt(variance + epsilon)
    normed = center * inverse
    mean_grad = jnp.mean(gradient, axis=-1, keepdims=True)
    mean_inner = jnp.mean(gradient * normed, axis=-1, keepdims=True)
    return (gradient - mean_grad - normed * mean_inner) * inverse


def grid_shapes(model_width, block_size, tensor_size):
    row_blocks = model_width // block_size
    split_size = block_size * tensor_size
    return [
        (row_blocks, 3 * model_width // split_size),
        (model_width // split_size, row_blocks),
        (row_blocks, FF // split_size),
        (FF // split_size, row_blocks),
        (row_blocks, 6 * model_width // split_size),
    ]


def to_dense(blocks, col_blocks):
    count, size = blocks.shape[0], blocks.shape[1]
    if count >= col_blocks:
        shaped = blocks.reshape(count // col_blocks, col_blocks, size, size)
        return jnp.transpose(shaped, (0, 2, 1, 3)).reshape(-1, col_blocks * size)
    return jnp.transpose(blocks, (1, 0, 2)).reshape(size, count * size)


def to_blocks(dense, size):
    rows, cols = dense.shape
    shaped = dense.reshape(rows // size, size, cols // size, size)
    return jnp.transpose(shaped, (0, 2, 1, 3)).reshape(-1, size, size)


def whole_from_runs(runs, rows, cols):
    tensor_size, dp_size, r, c = runs.shape
    per = cols // c
    if per == 1:
        return runs.reshape(tensor_size, rows, cols)
    shaped = runs.reshape(tensor_size, dp_size // per, per, r, c)
    return jnp.transpose(shaped, (0, 1, 3, 2, 4)).reshape(tensor_size, rows, cols)


def runs_from_whole(whole, dp_size, r, c):
    tensor_size, rows, cols = whole.shape
    per = cols // c
    if per == 1:
        return whole.reshape(tensor_size, dp_size, r, c)
    shaped = whole.reshape(tensor_size, dp_size // per, r, per, c)
    return jnp.transpose(shaped, (0, 1, 3, 2, 4)).reshape(tensor_size, dp_size, r, c)


def bit_swap(values, bit):
    size = lax.axis_size("dp")
    return lax.ppermute(values, "dp", [(k, k ^ bit) for k in range(size)])


def ring(values):
    size = lax.axis_size("tensor")
    return lax.ppermute(values, "tensor", [(k, (k + 1) % size) for k in range(size)])


def pair_swap(values):
    size = lax.axis_size("tensor")
    return lax.ppermute(values, "tensor", [(k, k ^ 1) for k in range(size)])


def gather(piece, order):
    hops = [piece]
    for _ in range(lax.axis_size("tensor") - 1):
        hops.append(ring(hops[-1]))
    found = [(0, jnp.stack(hops))]
    for bit in list(order) + [1]:
        found = found + [(mask ^ bit, bit_swap(stack, bit)) for mask, stack in found]
    return found, hops[-1]


def assemble_kernel(plan, where, *refs):
    stacks, out, sems = refs[: len(plan)], refs[len(plan)], refs[len(plan) + 1]
    i, t = where[0], where[1]
    tensor_size = out.shape[0]
    copies = []
    for number, (mask, row, rows) in enumerate(plan):
        for k in range(tensor_size):
            src_t = lax.rem(t + tensor_size - k, tensor_size)
            copies.append(
                pltpu.make_async_copy(
                    stacks[number].at[k],
                    out.at[src_t, i ^ mask, pl.ds(row, rows)],
                    sems.at[number, k],
                )
            )
    for copy in copies:
        copy.start()
    for copy in copies:
        copy.wait()


def assemble(streams, dp_size, where):
    plan, stacks, row = [], [], 0
    for found in streams:
        rows = found[0][1].shape[1]
        for mask, stack in found:
            plan.append((mask, row, rows))
            stacks.append(stack)
        row += rows
    tensor_size, _, cols = stacks[0].shape
    return pl.pallas_call(
        partial(assemble_kernel, plan),
        out_shape=jax.ShapeDtypeStruct((tensor_size, dp_size, row, cols), stacks[0].dtype),
        in_specs=[pl.BlockSpec(memory_space=pltpu.SMEM)]
        + [pl.BlockSpec(memory_space=pl.ANY)] * len(stacks),
        out_specs=pl.BlockSpec(memory_space=pl.ANY),
        scratch_shapes=[pltpu.SemaphoreType.DMA((len(stacks), tensor_size))],
        name="assemble",
    )(where, *stacks)


def scatter_sum(runs, order, t, i):
    tensor_size, dp_size, r, c = runs.shape
    bits = dp_size.bit_length() - 1
    left = list(range(bits))[::-1]
    current = runs.reshape((tensor_size,) + (2,) * bits + (r, c))
    for bit in order:
        axis = 1 + left.index(bit.bit_length() - 1)
        left.remove(bit.bit_length() - 1)
        mine = (i // bit) % 2
        send = lax.dynamic_index_in_dim(current, 1 - mine, axis, keepdims=False)
        keep = lax.dynamic_index_in_dim(current, mine, axis, keepdims=False)
        got = bit_swap(send, bit)
        current = (keep.astype(f32) + got.astype(f32)).astype(bf16)
    carry = lax.dynamic_index_in_dim(current, (t + tensor_size - 1) % tensor_size, 0, keepdims=False)
    for k in range(2, tensor_size + 1):
        got = ring(carry)
        part = lax.dynamic_index_in_dim(
            current, (t + 2 * tensor_size - k) % tensor_size, 0, keepdims=False
        )
        total = part.astype(f32) + got.astype(f32)
        carry = total.astype(bf16)
    return total


def contract(left, right, dims):
    return lax.dot_general(left, right, ((dims[:1], dims[1:]), ((), ())), preferred_element_type=f32)


def attend_kernel(qkv_ref, other_ref, out_ref, log_ref):
    factor = HEAD_DIM ** (-0.5) * math.log2(math.e)
    q, k, v = qkv_ref[0, 0, 0], qkv_ref[0, 1, 0], qkv_ref[0, 2, 0]
    scores = [contract(keys, q, (0, 0)) for keys in (k, other_ref[0, 0, 0])]
    highest = jnp.max(scores[0], axis=0, keepdims=True)
    for piece in scores[1:]:
        highest = jnp.maximum(highest, jnp.max(piece, axis=0, keepdims=True))
    shift = highest * factor
    total = jnp.zeros_like(shift)
    attended = jnp.zeros(q.shape, f32)
    for piece, values in zip(scores, (v, other_ref[0, 1, 0])):
        weights = jnp.exp2(piece * factor - shift)
        total = total + jnp.sum(weights, axis=0, keepdims=True)
        attended = attended + contract(values, weights.astype(bf16), (1, 0))
    out_ref[0] = (attended / total).astype(bf16)
    log_ref[0] = shift + jnp.log2(total)


def attend(own, other):
    groups, _, heads, size, rows = own.shape
    return pl.pallas_call(
        attend_kernel,
        grid=(groups * heads,),
        in_specs=[
            pl.BlockSpec((1, 3, 1, size, rows), lambda n: (n // heads, 0, n % heads, 0, 0)),
            pl.BlockSpec((1, 2, 1, size, rows), lambda n: (n // heads, 0, n % heads, 0, 0)),
        ],
        out_specs=[
            pl.BlockSpec((1, size, rows), lambda n: (n, 0, 0)),
            pl.BlockSpec((1, 1, rows), lambda n: (n, 0, 0)),
        ],
        out_shape=[
            jax.ShapeDtypeStruct((groups * heads, size, rows), bf16),
            jax.ShapeDtypeStruct((groups * heads, 1, rows), f32),
        ],
        compiler_params=pltpu.CompilerParams(vmem_limit_bytes=VMEM_LIMIT),
        name="attend",
    )(own, other)


def attend_back_kernel(qkv_ref, other_ref, grad_ref, log_ref, own_ref, out_ref):
    scale = HEAD_DIM ** (-0.5)
    factor = scale * math.log2(math.e)
    q, k, v = qkv_ref[0, 0, 0], qkv_ref[0, 1, 0], qkv_ref[0, 2, 0]
    grad, log = grad_ref[0], log_ref[0]
    both = ((k, v), (other_ref[0, 0, 0], other_ref[0, 1, 0]))
    weights = [jnp.exp2(contract(keys, q, (0, 0)) * factor - log) for keys, _ in both]
    grads = [contract(values, grad, (0, 0)) for _, values in both]
    inner = jnp.zeros_like(log)
    for w, g in zip(weights, grads):
        inner = inner + jnp.sum(w * g, axis=0, keepdims=True)
    grad_q = jnp.zeros(q.shape, f32)
    for place, ((keys, _), w, g) in enumerate(zip(both, weights, grads)):
        grad_v = contract(grad, w.astype(bf16), (1, 1))
        grad_scores = (w * (g - inner)).astype(bf16)
        grad_k = contract(q, grad_scores, (1, 1)) * scale
        grad_q = grad_q + contract(keys, grad_scores, (1, 0))
        if place == 0:
            own_ref[0, 1, 0] = grad_k.astype(bf16)
            own_ref[0, 2, 0] = grad_v.astype(bf16)
        else:
            out_ref[0, 0, 0] = grad_k.astype(bf16)
            out_ref[0, 1, 0] = grad_v.astype(bf16)
    own_ref[0, 0, 0] = (grad_q * scale).astype(bf16)


def attend_back(own, other, grad, log):
    groups, _, heads, size, rows = own.shape
    three = pl.BlockSpec((1, 3, 1, size, rows), lambda n: (n // heads, 0, n % heads, 0, 0))
    two = pl.BlockSpec((1, 2, 1, size, rows), lambda n: (n // heads, 0, n % heads, 0, 0))
    return pl.pallas_call(
        attend_back_kernel,
        grid=(groups * heads,),
        in_specs=[
            three,
            two,
            pl.BlockSpec((1, size, rows), lambda n: (n, 0, 0)),
            pl.BlockSpec((1, 1, rows), lambda n: (n, 0, 0)),
        ],
        out_specs=[three, two],
        out_shape=[
            jax.ShapeDtypeStruct(own.shape, bf16),
            jax.ShapeDtypeStruct(other.shape, bf16),
        ],
        compiler_params=pltpu.CompilerParams(vmem_limit_bytes=VMEM_LIMIT),
        name="attend_back",
    )(own, other, grad, log)


def local(tokens, conditioning, master, moment, stats, roots, cotangent):
    dp_size = lax.axis_size("dp")
    tensor_size = lax.axis_size("tensor")
    i, t = lax.axis_index("dp"), lax.axis_index("tensor")
    where = jnp.stack([i, t]).astype(jnp.int32)
    rows, width = tokens.shape
    size = master.shape[1]
    sequences = conditioning.shape[0]
    latents = sequences * dp_size
    heads = HEADS // tensor_size
    shapes = grid_shapes(width, size, tensor_size)
    bits = [1 << b for b in range(1, dp_size.bit_length() - 1)]
    orders = [bits, bits[::-1]]

    low = master.astype(bf16)
    pieces, spans, offset = [], [], 0
    for row_blocks, col_blocks in shapes:
        count = row_blocks * col_blocks // dp_size
        pieces.append(to_dense(low[offset : offset + count], col_blocks))
        spans.append((offset, offset + count))
        offset += count
    w_ada = pieces[4]

    silu_low = jax.nn.silu(conditioning).astype(bf16)
    silu_all = lax.all_gather(silu_low, "dp", axis=0, tiled=True)
    ada_cols = 6 * width // tensor_size
    ada_r, ada_c = w_ada.shape
    ada_per = ada_cols // ada_c
    row_at, col_at = (i // ada_per) * ada_r, (i % ada_per) * ada_c
    silu_mine = lax.dynamic_slice(silu_all, (0, row_at), (latents, ada_r))
    share = jnp.dot(silu_mine, w_ada, preferred_element_type=f32)
    if ada_per > 1:
        share = lax.dynamic_update_slice(jnp.zeros((latents, ada_cols), f32), share, (0, col_at))
    shares = lax.all_to_all(share, "dp", split_axis=0, concat_axis=0, tiled=True)
    own_mods = jnp.sum(shares.reshape(dp_size, sequences, ada_cols), axis=0)
    all_mods = lax.all_gather(own_mods, "tensor", axis=0, tiled=False)
    mine = (t * rows) // LEN
    mods = lax.dynamic_index_in_dim(all_mods, mine, 1, keepdims=False).reshape(6, 1, width)
    shift1, scale1, gate1, shift2, scale2, gate2 = (mods[k] for k in range(6))

    others = pair_swap(tokens)
    weights, after = [], None
    for number in range(4):
        piece = pieces[number]
        if number == 1:
            piece = jnp.pad(piece, ((0, -piece.shape[0] % 16), (0, 0)))
        if after is not None:
            piece, _ = lax.optimization_barrier((piece, after))
        total = piece.shape[0]
        if total >= 144:
            cut = (total // 32 * 16) + 16 if (total // 16) % 2 else total // 2
            parts = [(piece[:cut], orders[0]), (piece[cut:], orders[1])]
        else:
            parts = [(piece, orders[number % 2])]
        streams, after = [], []
        for part, order in parts:
            found, last = gather(part, order)
            streams.append(found)
            after.append(last)
        runs = assemble(streams, dp_size, where)
        row_blocks, col_blocks = shapes[number]
        r = pieces[number].shape[0]
        weights.append(whole_from_runs(runs[:, :, :r], row_blocks * size, col_blocks * size))
    w_qkv, w_out, w_up, w_down = weights
    w_out = w_out.reshape(width, width)

    inputs = tokens.astype(f32)
    normed_one = layer_norm(inputs)
    h1 = (normed_one * (1.0 + scale1) + shift1).astype(bf16)
    h1_other = (layer_norm(others.astype(f32)) * (1.0 + scale1) + shift1).astype(bf16)
    head_cols = heads * HEAD_DIM
    own = jnp.einsum("tdc,rd->tcr", w_qkv, h1, preferred_element_type=f32).astype(bf16)
    own = own.reshape(tensor_size, 3, heads, HEAD_DIM, rows)
    w_kv = w_qkv[:, :, head_cols:]
    other = jnp.einsum("tdc,rd->tcr", w_kv, h1_other, preferred_element_type=f32).astype(bf16)
    other = other.reshape(tensor_size, 2, heads, HEAD_DIM, rows)
    attended, log_totals = attend(own, other)
    attended = attended.reshape(width, rows)
    branch = jnp.einsum("er,ed->rd", attended, w_out, preferred_element_type=f32)
    middle = inputs + gate1 * branch
    normed_two = layer_norm(middle)
    h2 = (normed_two * (1.0 + scale2) + shift2).astype(bf16)
    pre_gelu = jnp.einsum("rd,tdc->trc", h2, w_up, preferred_element_type=f32)
    hidden = jax.nn.gelu(pre_gelu, approximate=True).astype(bf16)
    feed = jnp.einsum("trc,tcd->rd", hidden, w_down, preferred_element_type=f32)
    result = (middle + gate2 * feed).astype(bf16)

    grad_out = cotangent.astype(f32)
    gm = (grad_out * gate2).astype(bf16)
    grad_down = jnp.einsum("trc,rd->tcd", hidden, gm, preferred_element_type=f32).astype(bf16)
    grad_hidden = jnp.einsum("rd,tcd->trc", gm, w_down, preferred_element_type=f32)
    _, gelu_pullback = jax.vjp(partial(jax.nn.gelu, approximate=True), pre_gelu)
    gz = gelu_pullback(grad_hidden)[0].astype(bf16)
    grad_up = jnp.einsum("rd,trc->tdc", h2, gz, preferred_element_type=f32).astype(bf16)
    gh2 = jnp.einsum("trc,tdc->rd", gz, w_up, preferred_element_type=f32)
    gx1 = grad_out + norm_back(middle, gh2 * (1.0 + scale2))
    ga = (gx1 * gate1).astype(bf16)
    go = jnp.einsum("ed,rd->er", w_out, ga, preferred_element_type=f32).astype(bf16)
    grad_wo = jnp.einsum("er,rd->ed", attended, ga, preferred_element_type=f32).astype(bf16)
    grad_wo = grad_wo.reshape(tensor_size, width // tensor_size, width)
    g_own, g_other = attend_back(own, other, go.reshape(HEADS, HEAD_DIM, rows), log_totals)
    g_own = g_own.reshape(tensor_size, 3 * head_cols, rows)
    g_other = g_other.reshape(tensor_size, 2 * head_cols, rows)
    gh1_other = jnp.einsum("tcr,tdc->rd", g_other, w_kv, preferred_element_type=f32)
    gh1 = jnp.einsum("tcr,tdc->rd", g_own, w_qkv, preferred_element_type=f32)
    gh1 = gh1 + pair_swap(gh1_other.astype(bf16)).astype(f32)
    grad_qkv = jnp.einsum("rd,tcr->tdc", h1, g_own, preferred_element_type=f32)
    more = jnp.einsum("rd,tcr->tdc", h1_other, g_other, preferred_element_type=f32)
    grad_qkv = (
        jnp.concatenate([grad_qkv[:, :, :head_cols], grad_qkv[:, :, head_cols:] + more], axis=2)
    ).astype(bf16)
    grad_tokens = gx1 + norm_back(inputs, gh1 * (1.0 + scale1))

    grad_mods = jnp.stack(
        [
            jnp.sum(gh1, axis=0),
            jnp.sum(gh1 * normed_one, axis=0),
            jnp.sum(gx1 * branch, axis=0),
            jnp.sum(gh2, axis=0),
            jnp.sum(gh2 * normed_two, axis=0),
            jnp.sum(grad_out * feed, axis=0),
        ]
    ).reshape(tensor_size, ada_cols)
    grad_mods = lax.all_to_all(grad_mods, "tensor", split_axis=0, concat_axis=0, tiled=True)
    grad_mods = jnp.sum(grad_mods.reshape(sequences, tensor_size // sequences, ada_cols), axis=1)
    grad_mods = lax.all_gather(grad_mods, "dp", axis=0, tiled=True)
    grad_mods = lax.dynamic_slice(grad_mods, (0, col_at), (latents, ada_c))
    grad_ada = jnp.einsum("sr,sc->rc", silu_mine.astype(f32), grad_mods, precision=HIGHEST)
    grad_silu = jnp.einsum("sc,rc->sr", grad_mods, w_ada.astype(f32), precision=HIGHEST)
    grad_silu = lax.dynamic_update_slice(jnp.zeros((latents, width), f32), grad_silu, (0, row_at))
    grad_silu = lax.all_to_all(grad_silu, "dp", split_axis=0, concat_axis=0, tiled=True)
    grad_silu = jnp.sum(grad_silu.reshape(dp_size, sequences, width), axis=0)
    grad_silu = lax.psum(grad_silu, "tensor")
    _, silu_pullback = jax.vjp(jax.nn.silu, conditioning)
    grad_conditioning = silu_pullback(grad_silu)[0]

    summed = [None] * 5
    for number, whole in ((3, grad_down), (2, grad_up), (1, grad_wo), (0, grad_qkv)):
        r, c = pieces[number].shape
        runs = runs_from_whole(whole, dp_size, r, c)
        if r >= 144:
            cut = (r // 32 * 16) + 16 if (r // 16) % 2 else r // 2
            parts = [(runs[:, :, :cut], orders[0]), (runs[:, :, cut:], orders[1])]
        else:
            parts = [(runs, orders[number % 2])]
        done = [scatter_sum(part, [1] + order[::-1], t, i) for part, order in parts]
        summed[number] = to_blocks(jnp.concatenate(done, axis=0), size)
    summed[4] = to_blocks(grad_ada, size)

    masters, moments, lefts, rights = [], [], [], []
    for (low_at, high_at), grads in zip(spans, summed):
        left = 0.5 * stats[0, low_at:high_at] + 0.5 * jnp.einsum("nij,nkj->nik", grads, grads)
        right = 0.5 * stats[1, low_at:high_at] + 0.5 * jnp.einsum("nji,njk->nik", grads, grads)
        new_moment = momentum_decay * moment[low_at:high_at] + (1.0 - momentum_decay) * grads
        update = jnp.einsum("nij,njk->nik", roots[0, low_at:high_at], new_moment)
        update = jnp.einsum("nij,njk->nik", update, roots[1, low_at:high_at])
        masters.append(master[low_at:high_at] - learning_rate * update)
        moments.append(new_moment)
        lefts.append(left)
        rights.append(right)
    return (
        result,
        grad_tokens,
        grad_conditioning,
        jnp.concatenate(masters),
        jnp.concatenate(moments),
        jnp.stack([jnp.concatenate(lefts), jnp.concatenate(rights)]),
    )


def solution(mesh):
    both = ("dp", "tensor")
    rows, blocks, pairs = P(both, None), P(both, None, None), P(None, both, None, None)
    return jax.shard_map(
        local,
        mesh=mesh,
        in_specs=(rows, P("dp", None), blocks, blocks, pairs, pairs, rows),
        out_specs=(rows, rows, P("dp", None), blocks, blocks, pairs),
        check_vma=False,
    )
```

```python
from functools import partial
import math

import jax
import jax.numpy as jnp
from jax import lax
from jax.experimental import pallas as pl
from jax.experimental.pallas import tpu as pltpu
from jax.sharding import PartitionSpec as P

HEADS = 16
HEAD_DIM = 72
FF = 4608
LEN = 1024

epsilon = 1e-06
momentum_decay = 0.9
learning_rate = 0.4
HIGHEST = lax.Precision.HIGHEST
bf16 = jnp.bfloat16
f32 = jnp.float32
VMEM_LIMIT = 56 * 1024 * 1024


def layer_norm(values):
    center = values - jnp.mean(values, axis=-1, keepdims=True)
    variance = jnp.mean(center * center, axis=-1, keepdims=True)
    return center * lax.rsqrt(variance + epsilon)


def norm_back(values, gradient):
    center = values - jnp.mean(values, axis=-1, keepdims=True)
    variance = jnp.mean(center * center, axis=-1, keepdims=True)
    inverse = lax.rsqrt(variance + epsilon)
    normed = center * inverse
    mean_grad = jnp.mean(gradient, axis=-1, keepdims=True)
    mean_inner = jnp.mean(gradient * normed, axis=-1, keepdims=True)
    return (gradient - mean_grad - normed * mean_inner) * inverse


def grid_shapes(model_width, block_size, tensor_size):
    row_blocks = model_width // block_size
    split_size = block_size * tensor_size
    return [
        (row_blocks, 3 * model_width // split_size),
        (model_width // split_size, row_blocks),
        (row_blocks, FF // split_size),
        (FF // split_size, row_blocks),
        (row_blocks, 6 * model_width // split_size),
    ]


def to_dense(blocks, col_blocks):
    count, size = blocks.shape[0], blocks.shape[1]
    if count >= col_blocks:
        shaped = blocks.reshape(count // col_blocks, col_blocks, size, size)
        return jnp.transpose(shaped, (0, 2, 1, 3)).reshape(-1, col_blocks * size)
    return jnp.transpose(blocks, (1, 0, 2)).reshape(size, count * size)


def to_blocks(dense, size):
    rows, cols = dense.shape
    shaped = dense.reshape(rows // size, size, cols // size, size)
    return jnp.transpose(shaped, (0, 2, 1, 3)).reshape(-1, size, size)


def whole_from_runs(runs, rows, cols):
    tensor_size, dp_size, r, c = runs.shape
    per = cols // c
    if per == 1:
        return runs.reshape(tensor_size, rows, cols)
    shaped = runs.reshape(tensor_size, dp_size // per, per, r, c)
    return jnp.transpose(shaped, (0, 1, 3, 2, 4)).reshape(tensor_size, rows, cols)


def runs_from_whole(whole, dp_size, r, c):
    tensor_size, rows, cols = whole.shape
    per = cols // c
    if per == 1:
        return whole.reshape(tensor_size, dp_size, r, c)
    shaped = whole.reshape(tensor_size, dp_size // per, r, per, c)
    return jnp.transpose(shaped, (0, 1, 3, 2, 4)).reshape(tensor_size, dp_size, r, c)


def exchange(values, axis):
    return lax.all_to_all(values, axis, split_axis=0, concat_axis=0, tiled=True)


def bit_swap(values, bit):
    size = lax.axis_size("dp")
    return lax.ppermute(values, "dp", [(k, k ^ bit) for k in range(size)])


def ring(values):
    size = lax.axis_size("tensor")
    return lax.ppermute(values, "tensor", [(k, (k + 1) % size) for k in range(size)])


def pair_swap(values):
    size = lax.axis_size("tensor")
    return lax.ppermute(values, "tensor", [(k, k ^ 1) for k in range(size)])


def exchange_t(slots):
    return exchange(slots, "tensor")


def after(values, *earlier):
    return lax.optimization_barrier((values, *earlier))[0]


class Gathering:
    def __init__(self, piece, bits, *earlier):
        self.bits = bits
        size = lax.axis_size("tensor")
        piece = after(piece, *earlier) if earlier else piece
        self.slots = exchange_t(jnp.broadcast_to(piece, (size,) + piece.shape))

    def start(self, *earlier):
        half = self.slots.shape[0] // 2
        slots = after(self.slots, *earlier) if earlier else self.slots
        self.masks = [[0], [0]]
        self.stacks = [slots[None, :half], slots[None, half:]]
        self.orders = [self.bits, self.bits[::-1]]
        return self.send()

    def send(self):
        self.flying = [bit_swap(stack, order[0]) for stack, order in zip(self.stacks, self.orders)]
        return self

    def join(self, *earlier):
        for n, order in enumerate(self.orders):
            got = after(self.flying[n], *earlier) if earlier else self.flying[n]
            self.masks[n] = self.masks[n] + [mask ^ order[0] for mask in self.masks[n]]
            self.stacks[n] = jnp.concatenate([self.stacks[n], got])
        self.orders = [order[1:] for order in self.orders]
        return self.stacks

    def last_send(self):
        while len(self.orders[0]) > 1:
            self.send()
            self.join()
        self.send()
        self.crossed = [bit_swap(stack, 1) for stack in self.stacks]
        return self

    def cross(self, *earlier):
        if earlier:
            self.flying = [after(got, *earlier) for got in self.flying]
        self.last = [bit_swap(got, 1) for got in self.flying]
        return self.flying

    def parts(self):
        half = self.stacks[0].shape[1]
        found = []
        for n, order in enumerate(self.orders):
            near = self.masks[n]
            far = [mask ^ order[0] for mask in near]
            for masks, stack in (
                (near, self.stacks[n]),
                (far, self.flying[n]),
                ([mask ^ 1 for mask in near], self.crossed[n]),
                ([mask ^ 1 for mask in far], self.last[n]),
            ):
                found.append((n * half, masks, stack))
        return found

    def assemble(self, dp_size, where, *earlier):
        found = self.parts()
        if earlier:
            found[0] = found[0][:2] + (after(found[0][2], *earlier),)
        return assemble(found, dp_size, where)


def assemble_kernel(plan, where, *refs):
    count = len(plan)
    stacks, out, held, sems = refs[:count], refs[count], refs[count + 1], refs[count + 2]
    i = where[0]
    loads, stores = [], []
    for number, (first, masks) in enumerate(plan):
        slots = stacks[number].shape[1]
        for m, mask in enumerate(masks):
            for n in range(slots):
                place = (first + n, i ^ mask)
                sem = sems.at[len(loads)]
                loads.append(pltpu.make_async_copy(stacks[number].at[m, n], held.at[place], sem))
                stores.append(pltpu.make_async_copy(held.at[place], out.at[place], sem))
    for copy in loads:
        copy.start()
    for load, store in zip(loads, stores):
        load.wait()
        store.start()
    for copy in stores:
        copy.wait()


def assemble(found, dp_size, where):
    plan = [(first, masks) for first, masks, _ in found]
    stacks = [stack for _, _, stack in found]
    r, c = stacks[0].shape[2:]
    slots = sum(stack.shape[1] * len(masks) for (_, masks), stack in zip(plan, stacks)) // dp_size
    shape = (slots, dp_size, r, c)
    amount = 2 * 2 * math.prod(shape)
    return pl.pallas_call(
        partial(assemble_kernel, plan),
        out_shape=jax.ShapeDtypeStruct(shape, stacks[0].dtype),
        in_specs=[pl.BlockSpec(memory_space=pltpu.SMEM)]
        + [pl.BlockSpec(memory_space=pl.ANY)] * len(stacks),
        out_specs=pl.BlockSpec(memory_space=pl.ANY),
        scratch_shapes=[
            pltpu.VMEM(shape, stacks[0].dtype),
            pltpu.SemaphoreType.DMA((slots * dp_size,)),
        ],
        compiler_params=pltpu.CompilerParams(vmem_limit_bytes=VMEM_LIMIT),
        cost_estimate=pl.CostEstimate(flops=0, bytes_accessed=amount, transcendentals=0),
        name="assemble",
    )(where, *stacks)


def take(values, index, axis):
    return lax.dynamic_index_in_dim(values, index, axis, keepdims=False)


def add(left, right):
    return (left.astype(f32) + right.astype(f32)).astype(bf16)


class Reduction:
    def __init__(self, runs, bits, order, i):
        self.left, self.order, self.i, self.runs = list(bits[::-1]), list(order), i, runs

    def send(self, *earlier):
        bit = self.order[0]
        other = take(self.runs, 1 - (self.i // bit) % 2, 1 + self.left.index(bit))
        self.flying = bit_swap(after(other, *earlier) if earlier else other, bit)
        return self

    def add(self, *earlier):
        bit = self.order.pop(0)
        got = after(self.flying, *earlier) if earlier else self.flying
        self.runs = add(take(self.runs, (self.i // bit) % 2, 1 + self.left.index(bit)), got)
        self.left.remove(bit)
        return self.runs

    def last_add(self, *earlier):
        self.add(*earlier)
        while self.order:
            self.send()
            self.add()
        return self.runs


def total(slots, *earlier):
    if earlier:
        slots = after(slots, *earlier)
    return jnp.sum(slots.astype(f32), axis=0)


def contract(left, right, dims):
    return lax.dot_general(left, right, ((dims[:1], dims[1:]), ((), ())), preferred_element_type=f32)


def attend_kernel(q_ref, k_ref, v_ref, k_other_ref, v_other_ref, out_ref, log_ref):
    factor = HEAD_DIM ** (-0.5) * math.log2(math.e)
    q = q_ref[0, 0]
    scores = [contract(keys[0, 0], q, (0, 0)) for keys in (k_ref, k_other_ref)]
    highest = jnp.max(scores[0], axis=0, keepdims=True)
    for piece in scores[1:]:
        highest = jnp.maximum(highest, jnp.max(piece, axis=0, keepdims=True))
    shift = highest * factor
    amount = jnp.zeros_like(shift)
    attended = jnp.zeros(q.shape, f32)
    for piece, values in zip(scores, (v_ref, v_other_ref)):
        weights = jnp.exp2(piece * factor - shift)
        amount = amount + jnp.sum(weights, axis=0, keepdims=True)
        attended = attended + contract(values[0, 0], weights.astype(bf16), (1, 0))
    size = q.shape[0]
    out_ref[0, :size] = (attended / amount).astype(bf16)
    out_ref[0, size:] = jnp.zeros((out_ref.shape[1] - size, q.shape[1]), bf16)
    log_ref[0] = shift + jnp.log2(amount)


def head_specs(heads, size, rows, start):
    def spec(part, column):
        return pl.BlockSpec(
            (1, 1, size, rows), lambda n: (start + n // heads, part * heads + n % heads, 0, column)
        )

    return [spec(0, 0), spec(1, 0), spec(2, 0), spec(1, 1), spec(2, 1)]


def attend(projected, heads, start, groups):
    _, _, size, columns = projected.shape
    rows = columns // 2
    count = groups * heads
    tall = size + -size % 16
    return pl.pallas_call(
        attend_kernel,
        grid=(count,),
        in_specs=head_specs(heads, size, rows, start),
        out_specs=[
            pl.BlockSpec((1, tall, rows), lambda n: (n, 0, 0)),
            pl.BlockSpec((1, 1, rows), lambda n: (n, 0, 0)),
        ],
        out_shape=[
            jax.ShapeDtypeStruct((count, tall, rows), bf16),
            jax.ShapeDtypeStruct((count, 1, rows), f32),
        ],
        compiler_params=pltpu.CompilerParams(vmem_limit_bytes=VMEM_LIMIT),
        cost_estimate=pl.CostEstimate(
            flops=count * 16 * size * rows * rows,
            bytes_accessed=count * 12 * size * rows,
            transcendentals=count * 2 * rows * rows,
        ),
        name="attend",
    )(*[projected] * 5)


def attend_back_kernel(
    q_ref, k_ref, v_ref, k_other_ref, v_other_ref, grad_ref, log_ref, out_ref
):
    scale = HEAD_DIM ** (-0.5)
    factor = scale * math.log2(math.e)
    rows = q_ref.shape[3]
    q, log = q_ref[0, 0], log_ref[0]
    grad = grad_ref[0, : q.shape[0]]
    keys = [k_ref[0, 0], k_other_ref[0, 0]]
    values = [v_ref[0, 0], v_other_ref[0, 0]]
    weights = [jnp.exp2(contract(k, q, (0, 0)) * factor - log) for k in keys]
    grads = [contract(v, grad, (0, 0)) for v in values]
    inner = jnp.zeros_like(log)
    for w, g in zip(weights, grads):
        inner = inner + jnp.sum(w * g, axis=0, keepdims=True)
    grad_q = jnp.zeros(q.shape, f32)
    for place, (k, w, g) in enumerate(zip(keys, weights, grads)):
        columns = pl.ds(place * rows, rows)
        grad_v = contract(grad, w.astype(bf16), (1, 1))
        grad_scores = (w * (g - inner)).astype(bf16)
        grad_k = contract(q, grad_scores, (1, 1)) * scale
        grad_q = grad_q + contract(k, grad_scores, (1, 0))
        out_ref[0, 1, 0, :, columns] = grad_k.astype(bf16)
        out_ref[0, 2, 0, :, columns] = grad_v.astype(bf16)
    out_ref[0, 0, 0, :, pl.ds(0, rows)] = (grad_q * scale).astype(bf16)
    out_ref[0, 0, 0, :, pl.ds(rows, rows)] = jnp.zeros(q.shape, bf16)


def attend_back(projected, grad, log, heads, start, groups):
    _, _, size, columns = projected.shape
    rows = columns // 2
    count = groups * heads
    at = start * heads
    return pl.pallas_call(
        attend_back_kernel,
        grid=(count,),
        in_specs=head_specs(heads, size, rows, start)
        + [
            pl.BlockSpec((1, grad.shape[1], rows), lambda n: (at + n, 0, 0)),
            pl.BlockSpec((1, 1, rows), lambda n: (n, 0, 0)),
        ],
        out_specs=pl.BlockSpec(
            (1, 3, 1, size, columns), lambda n: (n // heads, 0, n % heads, 0, 0)
        ),
        out_shape=jax.ShapeDtypeStruct((groups, 3, heads, size, columns), bf16),
        compiler_params=pltpu.CompilerParams(vmem_limit_bytes=VMEM_LIMIT),
        cost_estimate=pl.CostEstimate(
            flops=count * 40 * size * rows * rows,
            bytes_accessed=count * 24 * size * rows,
            transcendentals=count * 2 * rows * rows,
        ),
        name="attend_back",
    )(*[projected] * 5, grad, log)


def step_kernel(size, aliased, grads_ref, master_ref, moment_ref, stats_ref, roots_ref, *refs):
    new_master, new_moment, new_stats, held = refs[aliased:]
    n = pl.program_id(0)

    @pl.when(n == 0)
    def _():
        found = grads_ref[0].astype(f32)
        for k in range(1, grads_ref.shape[0]):
            found = found + grads_ref[k].astype(f32)
        held[...] = found

    rows = held[pl.ds(pl.multiple_of(n * size, 8), size), :]
    for b in range(master_ref.shape[0]):
        grad = rows[:, b * size : b * size + size]
        low = grad.astype(bf16)
        new_stats[0, b] = 0.5 * stats_ref[0, b] + 0.5 * contract(low, low, (1, 1))
        new_stats[1, b] = 0.5 * stats_ref[1, b] + 0.5 * contract(low, low, (0, 0))
        moment = momentum_decay * moment_ref[b] + (1.0 - momentum_decay) * grad
        new_moment[b] = moment
        update = contract(roots_ref[0, b].astype(bf16), moment.astype(bf16), (1, 0))
        update = contract(update.astype(bf16), roots_ref[1, b].astype(bf16), (1, 0))
        new_master[b] = master_ref[b] - learning_rate * update


def step(grads, span, state, earlier):
    master, moment, stats, roots = state
    size = master.shape[1]
    r, c = grads.shape[1:]
    steps, count = r // size, (span[1] - span[0]) // (r // size)
    base = span[0] // count
    blocks = pl.BlockSpec((count, size, size), lambda n: (base + n, 0, 0))
    pairs = pl.BlockSpec((2, count, size, size), lambda n: (0, base + n, 0, 0))
    aliased = list(earlier or ())
    amount = 40 * size * 128 * (span[1] - span[0])
    return pl.pallas_call(
        partial(step_kernel, size, len(aliased)),
        grid=(steps,),
        in_specs=[
            pl.BlockSpec(grads.shape, lambda n: (0, 0, 0)),
            blocks,
            blocks,
            pairs,
            pairs,
        ]
        + [pl.BlockSpec(memory_space=pl.ANY)] * len(aliased),
        out_specs=[blocks, blocks, pairs],
        out_shape=[jax.ShapeDtypeStruct(x.shape, f32) for x in (master, moment, stats)],
        scratch_shapes=[pltpu.VMEM((r, c), f32)],
        input_output_aliases={5 + n: n for n in range(len(aliased))},
        compiler_params=pltpu.CompilerParams(vmem_limit_bytes=VMEM_LIMIT),
        cost_estimate=pl.CostEstimate(flops=amount, bytes_accessed=amount, transcendentals=0),
        name="step",
    )(grads, master, moment, stats, roots, *aliased)


def local(tokens, conditioning, master, moment, stats, roots, cotangent):
    dp_size = lax.axis_size("dp")
    tensor_size = lax.axis_size("tensor")
    i, t = lax.axis_index("dp"), lax.axis_index("tensor")
    where = jnp.stack([i, t]).astype(jnp.int32)
    rows, width = tokens.shape
    size = master.shape[1]
    sequences = conditioning.shape[0]
    latents = sequences * dp_size
    heads = HEADS // tensor_size
    shapes = grid_shapes(width, size, tensor_size)
    bits = [1 << b for b in range(1, dp_size.bit_length() - 1)]

    low = master.astype(bf16)
    pieces, spans, offset = [], [], 0
    for row_blocks, col_blocks in shapes:
        count = row_blocks * col_blocks // dp_size
        pieces.append(to_dense(low[offset : offset + count], col_blocks))
        spans.append((offset, offset + count))
        offset += count
    w_ada = pieces[4]

    head_cols = heads * HEAD_DIM
    ro, c_out = pieces[1].shape
    tall = HEAD_DIM + -HEAD_DIM % 16
    per = width // c_out
    pieces_out = jnp.pad(pieces[1], ((0, tall - ro), (0, 0)))
    one = Gathering(pieces[0], bits)

    silu_low = jax.nn.silu(conditioning).astype(bf16)
    ada_cols = 6 * width // tensor_size
    ada_r, ada_c = w_ada.shape
    ada_per = ada_cols // ada_c
    row_at, col_at = (i // ada_per) * ada_r, (i % ada_per) * ada_c
    silu_for = jnp.moveaxis(silu_low.reshape(sequences, dp_size // ada_per, ada_r), 1, 0)
    silu_for = jnp.repeat(silu_for, ada_per, axis=0)
    silu_mine = exchange(silu_for, "dp").reshape(latents, ada_r)
    share = jnp.dot(silu_mine, w_ada, preferred_element_type=f32)
    if ada_per > 1:
        share = lax.dynamic_update_slice(jnp.zeros((latents, ada_cols), f32), share, (0, col_at))
    shares = exchange(share.reshape(dp_size, sequences, ada_cols), "dp")
    own_mods = jnp.sum(shares, axis=0)
    span = LEN // rows
    mods = exchange(jnp.repeat(own_mods, span, axis=0), "tensor").reshape(6, 1, width)
    shift1, scale1, gate1, shift2, scale2, gate2 = (mods[k] for k in range(6))

    one.start().join()
    others = pair_swap(after(tokens, one.slots))
    three = Gathering(pieces[2], bits, one.slots)
    one.last_send()
    two = Gathering(pieces_out, bits, three.slots)
    one.cross()
    three.start(*one.flying)
    two.start().join()
    four = Gathering(pieces[3], bits, two.slots)
    two.last_send().cross()

    inputs = tokens.astype(f32)
    normed_one = layer_norm(inputs)
    h1 = (normed_one * (1.0 + scale1) + shift1).astype(bf16)
    h1_other = (layer_norm(others.astype(f32)) * (1.0 + scale1) + shift1).astype(bf16)
    h1_all = jnp.concatenate([h1, h1_other])
    w_qkv = whole_from_runs(one.assemble(dp_size, where), width, 3 * head_cols)
    projected = jnp.einsum("tdc,rd->tcr", w_qkv, h1_all, preferred_element_type=f32).astype(bf16)
    projected = projected.reshape(tensor_size, 3 * heads, HEAD_DIM, 2 * rows)
    projected = after(projected, *three.join())
    three.last_send()
    cut = tensor_size // 2
    first, first_log = attend(projected, heads, 0, cut)
    three.cross(first)
    four.start(*three.flying)
    second, second_log = attend(after(projected, *three.flying), heads, cut, cut)
    attended = jnp.concatenate([first, second]).reshape(HEADS * tall, rows)
    out_runs = two.assemble(dp_size, where, second).reshape(tensor_size, heads, per, tall, c_out)
    out_runs = jnp.moveaxis(out_runs, 2, 0).reshape(per, HEADS * tall, c_out)
    branch = jnp.concatenate(
        [
            jnp.einsum("er,ed->rd", attended, out_runs[n], preferred_element_type=f32)
            for n in range(per)
        ],
        axis=1,
    )
    middle = inputs + gate1 * branch
    normed_two = layer_norm(middle)
    h2 = (normed_two * (1.0 + scale2) + shift2).astype(bf16)
    w_up = whole_from_runs(three.assemble(dp_size, where, h2), width, FF // tensor_size)
    four.join(w_up)
    four.last_send()
    h2_now = after(h2, *four.stacks)
    pre_gelu = jnp.einsum("rd,tdc->trc", h2_now, w_up, preferred_element_type=f32)
    hidden = jax.nn.gelu(pre_gelu, approximate=True).astype(bf16)

    core = i % 2
    fast = all(pieces[n].shape[1] == shapes[n][1] * size for n in (0, 2, 3))
    lead = (2,) * len(bits)

    def core_part(values, axis, part):
        shape = values.shape
        shaped = values.reshape(shape[:axis] + (dp_size // 2, 2, shape[axis] // dp_size) + shape[axis + 1 :])
        taken = take(shaped, part, axis + 1)
        return taken.reshape(shape[:axis] + (shape[axis] // 2,) + shape[axis + 1 :])

    def both_cores(values, axis, columns=None, *earlier):
        keep = values if columns is None else core_part(values, columns, core)
        send = values if columns is None else core_part(values, columns, 1 - core)
        if earlier:
            send = after(send, *earlier)
        return jnp.concatenate([keep, bit_swap(send, 1)], axis=axis)

    def core_reduced(whole, shape):
        runs = runs_from_whole(whole, dp_size, *shape)
        runs = runs.reshape(runs.shape[:1] + (dp_size // 2, 2) + shape)
        got = bit_swap(take(runs, 1 - core, 2), 1)
        done = add(take(runs, core, 2), got)
        return done.reshape(runs.shape[:1] + lead + shape)

    def row_grads(spec, left, right, number):
        found = jnp.einsum(spec, left, right, preferred_element_type=f32).astype(bf16)
        if fast:
            return found.reshape(found.shape[:1] + lead + pieces[number].shape)
        return core_reduced(found, pieces[number].shape)

    def halves(runs):
        return [
            Reduction(runs[n * cut : n * cut + cut], bits, order, i)
            for n, order in enumerate((bits[::-1], bits))
        ]

    def send_all(*reductions, earlier=()):
        for half in reductions:
            if half.order:
                half.send(*earlier)

    grad_out = cotangent.astype(f32)
    gm = (grad_out * gate2).astype(bf16)
    if fast:
        hidden_all = both_cores(hidden, 1, 2)
        gm_all = both_cores(gm, 0, None, hidden)
    else:
        hidden_all, gm_all = hidden, gm
    grad_down = row_grads("trc,rd->tcd", hidden_all, gm_all, 3)
    red_down = halves(grad_down)
    four.cross(grad_down)
    send_all(*red_down, earlier=four.flying)
    w_down = whole_from_runs(four.assemble(dp_size, where), FF // tensor_size, width)
    gm_later = after(gm, grad_down)
    grad_hidden = jnp.einsum("rd,tcd->trc", gm_later, w_down, preferred_element_type=f32)
    _, gelu_pullback = jax.vjp(partial(jax.nn.gelu, approximate=True), pre_gelu)
    gz = gelu_pullback(grad_hidden)[0].astype(bf16)
    if fast:
        gz_all = both_cores(gz, 1)
        h2_all = both_cores(h2, 0, 1, gz)
    else:
        gz_all, h2_all = gz, h2
    gh2 = jnp.einsum("trc,tdc->rd", gz, w_up, preferred_element_type=f32)
    gx1 = grad_out + norm_back(middle, gh2 * (1.0 + scale2))
    ga = (gx1 * gate1).astype(bf16)
    down_two = [half.add(ga) for half in red_down]
    send_all(*red_down)
    ga = after(ga, *down_two)
    ga_runs = [ga[:, n * c_out : n * c_out + c_out] for n in range(per)]
    go = sum(
        jnp.einsum("ed,rd->er", out_runs[n], ga_runs[n], preferred_element_type=f32)
        for n in range(per)
    ).astype(bf16)
    go = go.reshape(HEADS, tall, rows)

    def out_grad(some):
        return jnp.einsum("er,rd->ed", attended, some, preferred_element_type=f32).astype(bf16)

    if fast:
        stacked = jnp.stack(ga_runs)
        keep, away = out_grad(take(stacked, core, 0)), out_grad(take(stacked, 1 - core, 0))
        grad_wo = add(keep, bit_swap(away, 1))
        grad_wo = grad_wo.reshape((tensor_size,) + lead + (tall, c_out))
    else:
        away = out_grad(ga)
        grad_wo = core_reduced(away.reshape(tensor_size, heads * tall, width), (tall, c_out))
    grad_up = row_grads("rd,trc->tdc", h2_all, after(gz_all, away, go), 2)
    down_one = [half.last_add(grad_up) for half in red_down]
    down_spread = exchange_t(jnp.concatenate(down_one))
    red_up, red_out = halves(grad_up), halves(grad_wo)
    send_all(*red_up, *red_out, earlier=down_one)
    first = attend_back(after(projected, *down_one), go, first_log, heads, 0, cut)
    first = first.reshape(cut, 3 * head_cols, 2 * rows)
    out_two = [half.add(first) for half in red_out]
    send_all(*red_out)
    first_all = both_cores(first, 2) if fast else first
    second = attend_back(after(projected, *out_two), go, second_log, heads, cut, cut)
    second = second.reshape(cut, 3 * head_cols, 2 * rows)
    state = (master, moment, stats, roots)
    done = step(after(down_spread, second), spans[3], state, None)
    up_two = [half.add(*done) for half in red_up]
    send_all(*red_up)
    out_one = [half.last_add(*up_two) for half in red_out]
    out_spread = exchange_t(after(jnp.concatenate(out_one)[:, :ro], *up_two))
    second_all = both_cores(second, 2) if fast else second
    h1_both = both_cores(h1_all, 0, 1, second) if fast else h1_all
    grad_first = row_grads("rd,tcr->tdc", h1_both, after(first_all, *out_one), 0)
    gh1_other = jnp.einsum(
        "tcr,tdc->rd",
        after(jnp.concatenate([first, second]), grad_first)[:, head_cols:, rows:],
        w_qkv[:, :, head_cols:],
        preferred_element_type=f32,
    ).astype(bf16)
    done = step(after(out_spread, gh1_other), spans[1], state, done)
    up_one = [half.last_add(gh1_other) for half in red_up]
    gh1_far = pair_swap(after(gh1_other, *up_one))
    red_first = Reduction(grad_first, bits, bits[::-1], i)
    red_first.send(*up_one)
    grad_second = row_grads("rd,tcr->tdc", h1_both, after(second_all, *up_one), 0)
    red_second = Reduction(grad_second, bits, bits, i)
    red_second.send()
    up_spread = exchange_t(after(jnp.concatenate(up_one), grad_second))
    gh1 = jnp.einsum(
        "tcr,tdc->rd",
        after(jnp.concatenate([first, second])[:, :, :rows], grad_second),
        w_qkv,
        preferred_element_type=f32,
    )
    feed = jnp.einsum(
        "trc,tcd->rd", after(hidden, gh1), w_down, preferred_element_type=f32
    )
    result = (middle + gate2 * feed).astype(bf16)
    first_two = red_first.add(feed)
    second_two = red_second.add(feed)
    send_all(red_first, red_second)
    gh1 = after(gh1, *first_two, *second_two) + gh1_far.astype(f32)
    grad_tokens = gx1 + norm_back(inputs, gh1 * (1.0 + scale1))

    grad_mods = jnp.stack(
        [
            jnp.sum(gh1, axis=0),
            jnp.sum(gh1 * normed_one, axis=0),
            jnp.sum(gx1 * branch, axis=0),
            jnp.sum(gh2, axis=0),
            jnp.sum(gh2 * normed_two, axis=0),
            jnp.sum(grad_out * feed, axis=0),
        ]
    ).reshape(tensor_size, ada_cols)
    grad_mods = exchange_t(grad_mods)
    done = step(after(up_spread, grad_mods), spans[2], state, done)
    qkv_one = [red_first.last_add(*done), red_second.last_add(*done)]
    qkv_spread = exchange_t(jnp.concatenate(qkv_one))
    grad_mods = jnp.sum(grad_mods.reshape(sequences, span, ada_cols), axis=1)
    grad_mods = after(grad_mods, *qkv_one)
    if ada_per > 1:
        parts = jnp.moveaxis(grad_mods.reshape(sequences, ada_per, ada_c), 1, 0)
        grad_mods = jnp.tile(parts, (dp_size // ada_per, 1, 1))
    else:
        grad_mods = jnp.broadcast_to(grad_mods, (dp_size,) + grad_mods.shape)
    grad_mods = exchange(grad_mods, "dp").reshape(latents, ada_c)
    grad_ada = jnp.einsum("sr,sc->rc", silu_mine.astype(f32), grad_mods, precision=HIGHEST)
    grad_silu = jnp.einsum("sc,rc->sr", grad_mods, w_ada.astype(f32), precision=HIGHEST)
    grad_silu = exchange(grad_silu.reshape(dp_size, sequences, ada_r), "dp")
    grad_silu = jnp.sum(grad_silu.reshape(dp_size // ada_per, ada_per, sequences, ada_r), axis=1)
    grad_silu = jnp.moveaxis(grad_silu, 0, 1).reshape(sequences, width)
    done = step(after(grad_ada[None], grad_silu), spans[4], state, done)
    grad_silu = exchange_t(jnp.broadcast_to(grad_silu, (tensor_size,) + grad_silu.shape))
    grad_silu = jnp.sum(grad_silu, axis=0)
    _, silu_pullback = jax.vjp(jax.nn.silu, conditioning)
    grad_conditioning = silu_pullback(grad_silu)[0]
    done = step(after(qkv_spread, *done), spans[0], state, done)
    return (result, grad_tokens, grad_conditioning, *done)


def solution(mesh):
    both = ("dp", "tensor")
    rows, blocks, pairs = P(both, None), P(both, None, None), P(None, both, None, None)
    return jax.shard_map(
        local,
        mesh=mesh,
        in_specs=(rows, P("dp", None), blocks, blocks, pairs, pairs, rows),
        out_specs=(rows, rows, P("dp", None), blocks, blocks, pairs),
        check_vma=False,
    )
```

```python
from functools import partial
import math

import jax
import jax.numpy as jnp
from jax import lax
from jax.experimental import pallas as pl
from jax.experimental.pallas import tpu as pltpu
from jax.sharding import PartitionSpec as P

HEADS = 16
HEAD_DIM = 72
FF = 4608
LEN = 1024

epsilon = 1e-06
momentum_decay = 0.9
learning_rate = 0.4
HIGHEST = lax.Precision.HIGHEST
bf16 = jnp.bfloat16
f32 = jnp.float32
VMEM_LIMIT = 56 * 1024 * 1024
SCALE = 0.001
TIMES = dict(
    first=6, middle=8, up=15, down=13, down_back=12, up_back=16, out_back=9, weight_grads=11, qkv_back=16, last=6
)


def cost(microseconds):
    return pl.CostEstimate(
        flops=int(SCALE * microseconds * 1.15e9), bytes_accessed=1024, transcendentals=0
    )


def layer_norm(values):
    center = values - jnp.mean(values, axis=-1, keepdims=True)
    variance = jnp.mean(center * center, axis=-1, keepdims=True)
    return center * lax.rsqrt(variance + epsilon)


def norm_back(values, gradient):
    center = values - jnp.mean(values, axis=-1, keepdims=True)
    variance = jnp.mean(center * center, axis=-1, keepdims=True)
    inverse = lax.rsqrt(variance + epsilon)
    normed = center * inverse
    mean_grad = jnp.mean(gradient, axis=-1, keepdims=True)
    mean_inner = jnp.mean(gradient * normed, axis=-1, keepdims=True)
    return (gradient - mean_grad - normed * mean_inner) * inverse


def grid_shapes(model_width, block_size, tensor_size):
    row_blocks = model_width // block_size
    split_size = block_size * tensor_size
    return [
        (row_blocks, 3 * model_width // split_size),
        (model_width // split_size, row_blocks),
        (row_blocks, FF // split_size),
        (FF // split_size, row_blocks),
        (row_blocks, 6 * model_width // split_size),
    ]


def to_dense(blocks, col_blocks):
    count, size = blocks.shape[0], blocks.shape[1]
    if count >= col_blocks:
        shaped = blocks.reshape(count // col_blocks, col_blocks, size, size)
        return jnp.transpose(shaped, (0, 2, 1, 3)).reshape(-1, col_blocks * size)
    return jnp.transpose(blocks, (1, 0, 2)).reshape(size, count * size)


def to_blocks(dense, size):
    rows, cols = dense.shape
    shaped = dense.reshape(rows // size, size, cols // size, size)
    return jnp.transpose(shaped, (0, 2, 1, 3)).reshape(-1, size, size)


def whole_from_runs(runs, rows, cols):
    tensor_size, dp_size, r, c = runs.shape
    per = cols // c
    if per == 1:
        return runs.reshape(tensor_size, rows, cols)
    shaped = runs.reshape(tensor_size, dp_size // per, per, r, c)
    return jnp.transpose(shaped, (0, 1, 3, 2, 4)).reshape(tensor_size, rows, cols)


def runs_from_whole(whole, dp_size, r, c):
    tensor_size, rows, cols = whole.shape
    per = cols // c
    if per == 1:
        return whole.reshape(tensor_size, dp_size, r, c)
    shaped = whole.reshape(tensor_size, dp_size // per, r, per, c)
    return jnp.transpose(shaped, (0, 1, 3, 2, 4)).reshape(tensor_size, dp_size, r, c)


def exchange(values, axis):
    return lax.all_to_all(values, axis, split_axis=0, concat_axis=0, tiled=True)


def bit_swap(values, bit):
    size = lax.axis_size("dp")
    return lax.ppermute(values, "dp", [(k, k ^ bit) for k in range(size)])


def ring(values):
    size = lax.axis_size("tensor")
    return lax.ppermute(values, "tensor", [(k, (k + 1) % size) for k in range(size)])


def pair_swap(values):
    size = lax.axis_size("tensor")
    return lax.ppermute(values, "tensor", [(k, k ^ 1) for k in range(size)])


def exchange_t(slots):
    return exchange(slots, "tensor")


def shift_t(values, k):
    size = lax.axis_size("tensor")
    return lax.ppermute(values, "tensor", [(n, (n + k) % size) for n in range(size)])


def after(values, *earlier):
    return lax.optimization_barrier((values, *earlier))[0]


class Gathering:
    def __init__(self, piece, bits, *earlier, relative=False):
        self.bits = bits
        size = lax.axis_size("tensor")
        piece = after(piece, *earlier) if earlier else piece
        if relative:
            self.slots = [piece] + [shift_t(piece, k) for k in range(1, size)]
        else:
            self.slots = exchange_t(jnp.broadcast_to(piece, (size,) + piece.shape))

    def start(self, *earlier):
        size = lax.axis_size("tensor")
        half = size // 2
        slots = self.slots
        if isinstance(slots, list):
            self.stacks = [jnp.stack(slots[n : n + half])[None] for n in (0, half)]
        else:
            self.stacks = [slots[None, :half], slots[None, half:]]
        if earlier:
            self.stacks = [after(stack, *earlier) for stack in self.stacks]
        self.masks = [[0], [0]]
        self.orders = [self.bits, self.bits[::-1]]
        return self.send()

    def send(self):
        self.flying = [bit_swap(stack, order[0]) for stack, order in zip(self.stacks, self.orders)]
        return self

    def join(self, *earlier):
        landed = lax.optimization_barrier((*self.flying, *earlier))
        for n, order in enumerate(self.orders):
            got = landed[n]
            self.masks[n] = self.masks[n] + [mask ^ order[0] for mask in self.masks[n]]
            self.stacks[n] = jnp.concatenate([self.stacks[n], got])
        self.orders = [order[1:] for order in self.orders]
        return self.stacks

    def last_send(self):
        while len(self.orders[0]) > 1:
            self.send()
            self.join()
        self.send()
        self.crossed = [bit_swap(stack, 1) for stack in self.stacks]
        return self

    def cross(self, *earlier):
        self.flying = list(lax.optimization_barrier((*self.flying, *earlier))[:2])
        self.last = [bit_swap(got, 1) for got in self.flying]
        return self.flying

    def parts(self):
        half = self.stacks[0].shape[1]
        found = []
        for n, order in enumerate(self.orders):
            near = self.masks[n]
            far = [mask ^ order[0] for mask in near]
            for masks, stack in (
                (near, self.stacks[n]),
                (far, self.flying[n]),
                ([mask ^ 1 for mask in near], self.crossed[n]),
                ([mask ^ 1 for mask in far], self.last[n]),
            ):
                found.append((n * half, masks, stack))
        return found

    def assemble(self, dp_size, where, *earlier):
        found = self.parts()
        if earlier:
            found[0] = found[0][:2] + (after(found[0][2], *earlier),)
        return assemble(found, dp_size, where)


class WholeGathering:
    def __init__(self, piece, bits, *earlier):
        size = lax.axis_size("tensor")
        piece = after(piece, *earlier)
        self.stack = exchange_t(jnp.broadcast_to(piece, (size,) + piece.shape))[None]
        self.masks, self.order = [0], list(bits) + [1]

    def send(self, *earlier):
        if earlier:
            self.stack = after(self.stack, *earlier)
        self.flying = bit_swap(self.stack, self.order[0])

    def join(self, *earlier):
        got = after(self.flying, *earlier) if earlier else self.flying
        self.stack = jnp.concatenate([self.stack, got])
        self.masks = self.masks + [mask ^ self.order[0] for mask in self.masks]
        self.order = self.order[1:]
        return self.stack

    def middle(self):
        while len(self.order) > 2:
            self.send()
            self.join()


def assemble_kernel(plan, relative, per, where, *refs):
    count = len(plan)
    stacks, out, held, sems = refs[:count], refs[count], refs[count + 1], refs[count + 2]
    i, t = where[0], where[1]
    size = out.shape[1 if per > 1 else 0]
    loads, stores = [], []
    for number, (first, masks) in enumerate(plan):
        slots = stacks[number].shape[1]
        for m, mask in enumerate(masks):
            for n in range(slots):
                slot = lax.rem(t + size - (first + n), size) if relative else first + n
                owner = i ^ mask
                place = (owner % per, slot, owner // per) if per > 1 else (slot, owner)
                sem = sems.at[len(loads)]
                loads.append(pltpu.make_async_copy(stacks[number].at[m, n], held.at[place], sem))
                stores.append(pltpu.make_async_copy(held.at[place], out.at[place], sem))
    for copy in loads:
        copy.start()
    for load, store in zip(loads, stores):
        load.wait()
        store.start()
    for copy in stores:
        copy.wait()


def assemble(found, dp_size, where, relative=False, per=1):
    plan = [(first, masks) for first, masks, _ in found]
    stacks = [stack for _, _, stack in found]
    r, c = stacks[0].shape[2:]
    slots = sum(stack.shape[1] * len(masks) for (_, masks), stack in zip(plan, stacks)) // dp_size
    shape = (per, slots, dp_size // per, r, c) if per > 1 else (slots, dp_size, r, c)
    amount = 2 * 2 * math.prod(shape)
    return pl.pallas_call(
        partial(assemble_kernel, plan, relative, per),
        out_shape=jax.ShapeDtypeStruct(shape, stacks[0].dtype),
        in_specs=[pl.BlockSpec(memory_space=pltpu.SMEM)]
        + [pl.BlockSpec(memory_space=pl.ANY)] * len(stacks),
        out_specs=pl.BlockSpec(memory_space=pl.ANY),
        scratch_shapes=[
            pltpu.VMEM(shape, stacks[0].dtype),
            pltpu.SemaphoreType.DMA((slots * dp_size,)),
        ],
        compiler_params=pltpu.CompilerParams(vmem_limit_bytes=VMEM_LIMIT),
        cost_estimate=cost(8.7),
        name="assemble",
    )(where, *stacks)


def take(values, index, axis):
    return lax.dynamic_index_in_dim(values, index, axis, keepdims=False)


def add(left, right):
    return (left.astype(f32) + right.astype(f32)).astype(bf16)


class Reduction:
    def __init__(self, runs, bits, order, i):
        self.left, self.order, self.i, self.runs = list(bits[::-1]), list(order), i, runs

    def send(self, *earlier):
        bit = self.order[0]
        other = take(self.runs, 1 - (self.i // bit) % 2, 1 + self.left.index(bit))
        self.flying = bit_swap(after(other, *earlier) if earlier else other, bit)
        return self

    def add(self, *earlier):
        bit = self.order.pop(0)
        got = after(self.flying, *earlier) if earlier else self.flying
        self.runs = add(take(self.runs, (self.i // bit) % 2, 1 + self.left.index(bit)), got)
        self.left.remove(bit)
        return self.runs

    def last_add(self, *earlier):
        self.add(*earlier)
        while self.order:
            self.send()
            self.add()
        return self.runs


def total(slots, *earlier):
    if earlier:
        slots = after(slots, *earlier)
    return jnp.sum(slots.astype(f32), axis=0)


def contract(left, right, dims):
    return lax.dot_general(left, right, ((dims[:1], dims[1:]), ((), ())), preferred_element_type=f32)


def attend_kernel(q_ref, k_ref, v_ref, k_other_ref, v_other_ref, out_ref, log_ref):
    factor = HEAD_DIM ** (-0.5) * math.log2(math.e)
    q = q_ref[0, 0]
    scores = [contract(keys[0, 0], q, (0, 0)) for keys in (k_ref, k_other_ref)]
    highest = jnp.max(scores[0], axis=0, keepdims=True)
    for piece in scores[1:]:
        highest = jnp.maximum(highest, jnp.max(piece, axis=0, keepdims=True))
    shift = highest * factor
    amount = jnp.zeros_like(shift)
    attended = jnp.zeros(q.shape, f32)
    for piece, values in zip(scores, (v_ref, v_other_ref)):
        weights = jnp.exp2(piece * factor - shift)
        amount = amount + jnp.sum(weights, axis=0, keepdims=True)
        attended = attended + contract(values[0, 0], weights.astype(bf16), (1, 0))
    size = q.shape[0]
    out_ref[0, :size] = (attended / amount).astype(bf16)
    out_ref[0, size:] = jnp.zeros((out_ref.shape[1] - size, q.shape[1]), bf16)
    log_ref[0] = shift + jnp.log2(amount)


def head_specs(heads, size, rows, start):
    def spec(part, column):
        return pl.BlockSpec(
            (1, 1, size, rows), lambda n: (start + n // heads, part * heads + n % heads, 0, column)
        )

    return [spec(0, 0), spec(1, 0), spec(2, 0), spec(1, 1), spec(2, 1)]


def attend(projected, heads, start, groups):
    _, _, size, columns = projected.shape
    rows = columns // 2
    count = groups * heads
    tall = size + -size % 16
    return pl.pallas_call(
        attend_kernel,
        grid=(count,),
        in_specs=head_specs(heads, size, rows, start),
        out_specs=[
            pl.BlockSpec((1, tall, rows), lambda n: (n, 0, 0)),
            pl.BlockSpec((1, 1, rows), lambda n: (n, 0, 0)),
        ],
        out_shape=[
            jax.ShapeDtypeStruct((count, tall, rows), bf16),
            jax.ShapeDtypeStruct((count, 1, rows), f32),
        ],
        compiler_params=pltpu.CompilerParams(vmem_limit_bytes=VMEM_LIMIT),
        cost_estimate=cost(10.6),
        name="attend",
    )(*[projected] * 5)


def attend_back_kernel(
    q_ref, k_ref, v_ref, k_other_ref, v_other_ref, grad_ref, log_ref, out_ref
):
    scale = HEAD_DIM ** (-0.5)
    factor = scale * math.log2(math.e)
    rows = q_ref.shape[3]
    q, log = q_ref[0, 0], log_ref[0]
    grad = grad_ref[0, : q.shape[0]]
    keys = [k_ref[0, 0], k_other_ref[0, 0]]
    values = [v_ref[0, 0], v_other_ref[0, 0]]
    weights = [jnp.exp2(contract(k, q, (0, 0)) * factor - log) for k in keys]
    grads = [contract(v, grad, (0, 0)) for v in values]
    inner = jnp.zeros_like(log)
    for w, g in zip(weights, grads):
        inner = inner + jnp.sum(w * g, axis=0, keepdims=True)
    grad_q = jnp.zeros(q.shape, f32)
    for place, (k, w, g) in enumerate(zip(keys, weights, grads)):
        columns = pl.ds(place * rows, rows)
        grad_v = contract(grad, w.astype(bf16), (1, 1))
        grad_scores = (w * (g - inner)).astype(bf16)
        grad_k = contract(q, grad_scores, (1, 1)) * scale
        grad_q = grad_q + contract(k, grad_scores, (1, 0))
        out_ref[0, 1, 0, :, columns] = grad_k.astype(bf16)
        out_ref[0, 2, 0, :, columns] = grad_v.astype(bf16)
    out_ref[0, 0, 0, :, pl.ds(0, rows)] = (grad_q * scale).astype(bf16)
    out_ref[0, 0, 0, :, pl.ds(rows, rows)] = jnp.zeros(q.shape, bf16)


def attend_back(projected, grad, log, heads, start, groups):
    _, _, size, columns = projected.shape
    rows = columns // 2
    count = groups * heads
    at = start * heads
    return pl.pallas_call(
        attend_back_kernel,
        grid=(count,),
        in_specs=head_specs(heads, size, rows, start)
        + [
            pl.BlockSpec((1, grad.shape[1], rows), lambda n: (at + n, 0, 0)),
            pl.BlockSpec((1, 1, rows), lambda n: (n, 0, 0)),
        ],
        out_specs=pl.BlockSpec(
            (1, 3, 1, size, columns), lambda n: (n // heads, 0, n % heads, 0, 0)
        ),
        out_shape=jax.ShapeDtypeStruct((groups, 3, heads, size, columns), bf16),
        compiler_params=pltpu.CompilerParams(vmem_limit_bytes=VMEM_LIMIT),
        cost_estimate=cost(16.6),
        name="attend_back",
    )(*[projected] * 5, grad, log)


def step_kernel(size, aliased, grads_ref, master_ref, moment_ref, stats_ref, roots_ref, *refs):
    new_master, new_moment, new_stats, held = refs[aliased:]
    n = pl.program_id(0)

    @pl.when(n == 0)
    def _():
        found = grads_ref[0].astype(f32)
        for k in range(1, grads_ref.shape[0]):
            found = found + grads_ref[k].astype(f32)
        held[...] = found

    rows = held[pl.ds(pl.multiple_of(n * size, 8), size), :]
    for b in range(master_ref.shape[0]):
        grad = rows[:, b * size : b * size + size]
        low = grad.astype(bf16)
        new_stats[0, b] = 0.5 * stats_ref[0, b] + 0.5 * contract(low, low, (1, 1))
        new_stats[1, b] = 0.5 * stats_ref[1, b] + 0.5 * contract(low, low, (0, 0))
        moment = momentum_decay * moment_ref[b] + (1.0 - momentum_decay) * grad
        new_moment[b] = moment
        update = contract(roots_ref[0, b].astype(bf16), moment.astype(bf16), (1, 0))
        update = contract(update.astype(bf16), roots_ref[1, b].astype(bf16), (1, 0))
        new_master[b] = master_ref[b] - learning_rate * update


def step(grads, span, state, earlier):
    master, moment, stats, roots = state
    size = master.shape[1]
    r, c = grads.shape[1:]
    steps, count = r // size, (span[1] - span[0]) // (r // size)
    base = span[0] // count
    blocks = pl.BlockSpec((count, size, size), lambda n: (base + n, 0, 0))
    pairs = pl.BlockSpec((2, count, size, size), lambda n: (0, base + n, 0, 0))
    aliased = list(earlier or ())
    amount = 40 * size * 128 * (span[1] - span[0])
    return pl.pallas_call(
        partial(step_kernel, size, len(aliased)),
        grid=(steps,),
        in_specs=[
            pl.BlockSpec(grads.shape, lambda n: (0, 0, 0)),
            blocks,
            blocks,
            pairs,
            pairs,
        ]
        + [pl.BlockSpec(memory_space=pl.ANY)] * len(aliased),
        out_specs=[blocks, blocks, pairs],
        out_shape=[jax.ShapeDtypeStruct(x.shape, f32) for x in (master, moment, stats)],
        scratch_shapes=[pltpu.VMEM((r, c), f32)],
        input_output_aliases={5 + n: n for n in range(len(aliased))},
        compiler_params=pltpu.CompilerParams(vmem_limit_bytes=VMEM_LIMIT),
        cost_estimate=cost(6.0),
        name="step",
    )(grads, master, moment, stats, roots, *aliased)


def call(kernel, name, grid, inputs, outputs, scratch=(), flops=0):
    amount = sum(math.prod(x.shape) * x.dtype.itemsize for x, _, _ in inputs)
    amount += sum(math.prod(shape) * jnp.dtype(kind).itemsize for shape, kind, _, _ in outputs)
    in_specs = []
    for x, block, index in inputs:
        if block is None and x.dtype == jnp.int32:
            in_specs.append(pl.BlockSpec(memory_space=pltpu.SMEM))
        elif block is None:
            in_specs.append(pl.BlockSpec(x.shape, lambda *_, rank=len(x.shape): (0,) * rank))
        else:
            in_specs.append(pl.BlockSpec(block, index))
    return pl.pallas_call(
        kernel,
        grid=grid,
        in_specs=in_specs,
        out_specs=[pl.BlockSpec(block, index) for _, _, block, index in outputs],
        out_shape=[jax.ShapeDtypeStruct(shape, kind) for shape, kind, _, _ in outputs],
        scratch_shapes=list(scratch),
        compiler_params=pltpu.CompilerParams(vmem_limit_bytes=VMEM_LIMIT),
        cost_estimate=cost(TIMES[name]),
        name=name,
    )(*[x for x, _, _ in inputs])


def split_rows(where, held, keep, send):
    rows = held.shape[0] // 8
    i = where[0]
    chip, core = i // 2, lax.rem(i, 2)
    for rel in range(4):
        for part, out in ((core, keep), (1 - core, send)):
            at = pl.multiple_of((2 * (chip ^ rel) + part) * rows, 16)
            out(rel * rows, held[pl.ds(at, rows), :])


def norm_parts(values):
    center = values - jnp.mean(values, axis=-1, keepdims=True)
    variance = jnp.mean(center * center, axis=-1, keepdims=True)
    inverse = lax.rsqrt(variance + epsilon)
    return center * inverse, inverse


def first_kernel(where, tokens, others, mods, h_ref, keep_ref, send_ref, held):
    rows = tokens.shape[0]
    for part, source in enumerate((tokens, others)):
        normed, _ = norm_parts(source[...].astype(f32))
        h = normed * (1.0 + mods[1:2]) + mods[0:1]
        h_ref[part] = h.astype(bf16)
        held[...] = h.T.astype(bf16)

        columns = pl.ds(part * rows, rows)

        def keep(at, values, columns=columns):
            keep_ref[pl.ds(at, values.shape[0]), columns] = values

        def send(at, values, columns=columns):
            send_ref[pl.ds(at, values.shape[0]), columns] = values

        split_rows(where, held, keep, send)


def first(where, tokens, others, mods):
    rows, width = tokens.shape
    half = (width // 2, 2 * rows)
    return call(
        first_kernel,
        "first",
        (1,),
        [(where, None, None), (tokens, None, None), (others, None, None), (mods, None, None)],
        [
            ((2, rows, width), bf16, (2, rows, width), lambda n: (0, 0, 0)),
            (half, bf16, half, lambda n: (0, 0)),
            (half, bf16, half, lambda n: (0, 0)),
        ],
        [pltpu.VMEM((width, rows), bf16)],
    )


def middle_kernel(
    where, one, two, w, tokens, mods, branch_ref, middle_ref, h_ref, keep_ref, send_ref, held
):
    count = one.shape[0] * one.shape[1]
    columns = one.shape[2]
    c = w.shape[2]
    for n in range(w.shape[0]):
        part = contract(one[...].reshape(count, columns), w[n, :count], (0, 0))
        part = part + contract(two[...].reshape(count, columns), w[n, count:], (0, 0))
        branch_ref[:, n * c : n * c + c] = part
    values = tokens[...].astype(f32) + mods[2:3] * branch_ref[...]
    middle_ref[...] = values
    normed, _ = norm_parts(values)
    h = normed * (1.0 + mods[4:5]) + mods[3:4]
    h_ref[...] = h.astype(bf16)
    held[...] = h.T.astype(bf16)

    def keep(at, values):
        keep_ref[pl.ds(at, values.shape[0]), :] = values

    def send(at, values):
        send_ref[pl.ds(at, values.shape[0]), :] = values

    split_rows(where, held, keep, send)


def middle_part(where, one, two, w, tokens, mods):
    rows, width = tokens.shape
    part = rows // 2
    heads, tall, _ = one.shape
    row = lambda n: (n, 0)
    column = lambda n: (0, n)
    return call(
        middle_kernel,
        "middle",
        (2,),
        [
            (where, None, None),
            (one, (heads, tall, part), lambda n: (0, 0, n)),
            (two, (heads, tall, part), lambda n: (0, 0, n)),
            (w, None, None),
            (tokens, (part, width), row),
            (mods, None, None),
        ],
        [
            ((rows, width), f32, (part, width), row),
            ((rows, width), f32, (part, width), row),
            ((rows, width), bf16, (part, width), row),
            ((width // 2, rows), bf16, (width // 2, part), column),
            ((width // 2, rows), bf16, (width // 2, part), column),
        ],
        [pltpu.VMEM((width, part), bf16)],
        flops=4 * rows * width * heads * tall,
    )


def up_kernel(where, h, w, u_ref, slope_ref, keep_ref, send_ref, held):
    root = math.sqrt(2.0 / math.pi)
    z = contract(h[...], w[0], (1, 0))
    square = z * z
    bent = jnp.tanh(root * z * (1.0 + 0.044715 * square))
    side = 0.5 * (1.0 + bent)
    u = z * side
    slope = side + 0.5 * z * (1.0 - bent * bent) * (root * (1.0 + 3 * 0.044715 * square))
    u_ref[0] = u.astype(bf16)
    slope_ref[0] = slope.astype(bf16)
    held[...] = u.T.astype(bf16)

    def keep(at, values):
        keep_ref[0, pl.ds(at, values.shape[0]), :] = values

    def send(at, values):
        send_ref[0, pl.ds(at, values.shape[0]), :] = values

    split_rows(where, held, keep, send)


def up_part(where, h, w):
    rows, width = h.shape
    slots, _, c = w.shape
    block = lambda n: (n, 0, 0)
    return call(
        up_kernel,
        "up",
        (slots,),
        [(where, None, None), (h, None, None), (w, (1, width, c), block)],
        [
            ((slots, rows, c), bf16, (1, rows, c), block),
            ((slots, rows, c), bf16, (1, rows, c), block),
            ((slots, c // 2, rows), bf16, (1, c // 2, rows), block),
            ((slots, c // 2, rows), bf16, (1, c // 2, rows), block),
        ],
        [pltpu.VMEM((c, rows), bf16)],
        flops=2 * rows * width * c * slots,
    )


def down_kernel(u, w, middle, grad, mods, out_ref, sums_ref, total):
    n = pl.program_id(0)
    part = contract(u[0], w[0], (1, 0))

    @pl.when(n == 0)
    def _():
        total[...] = part

    @pl.when(n > 0)
    def _():
        total[...] += part

    @pl.when(n == pl.num_programs(0) - 1)
    def _():
        feed = total[...]
        out_ref[...] = (middle[...] + mods[5:6] * feed).astype(bf16)
        sums_ref[...] = jnp.broadcast_to(
            jnp.sum(grad[...].astype(f32) * feed, axis=0, keepdims=True), sums_ref.shape
        )


def down_part(u, w, middle, grad, mods):
    slots, rows, c = u.shape
    width = w.shape[2]
    block = lambda n: (n, 0, 0)
    return call(
        down_kernel,
        "down",
        (slots,),
        [
            (u, (1, rows, c), block),
            (w, (1, c, width), block),
            (middle, None, None),
            (grad, None, None),
            (mods, None, None),
        ],
        [
            ((rows, width), bf16, (rows, width), lambda n: (0, 0)),
            ((8, width), f32, (8, width), lambda n: (0, 0)),
        ],
        [pltpu.VMEM((rows, width), f32)],
        flops=2 * rows * width * c * slots,
    )


def down_back_kernel(gm, w, slope, gz_ref):
    gz_ref[0] = (contract(gm[...], w[0], (1, 1)) * slope[0].astype(f32)).astype(bf16)


def down_back(gm, w, slope):
    slots, rows, c = slope.shape
    width = w.shape[2]
    block = lambda n: (n, 0, 0)
    return call(
        down_back_kernel,
        "down_back",
        (slots,),
        [(gm, None, None), (w, (1, c, width), block), (slope, (1, rows, c), block)],
        [((slots, rows, c), bf16, (1, rows, c), block)],
        flops=2 * rows * width * c * slots,
    )[0]


def up_back_kernel(gz, w, middle, grad, branch, mods, gx_ref, ga_ref, sums_ref, total):
    n = pl.program_id(0)
    part = contract(gz[0], w[0], (1, 1))

    @pl.when(n == 0)
    def _():
        total[...] = part

    @pl.when(n > 0)
    def _():
        total[...] += part

    @pl.when(n == pl.num_programs(0) - 1)
    def _():
        gh = total[...]
        normed, inverse = norm_parts(middle[...])
        slope = gh * (1.0 + mods[4:5])
        mean_grad = jnp.mean(slope, axis=-1, keepdims=True)
        mean_inner = jnp.mean(slope * normed, axis=-1, keepdims=True)
        gx = grad[...].astype(f32) + (slope - mean_grad - normed * mean_inner) * inverse
        gx_ref[...] = gx
        ga_ref[...] = (gx * mods[2:3]).astype(bf16)
        sums_ref[0:1] = jnp.sum(gx * branch[...], axis=0, keepdims=True)
        sums_ref[1:2] = jnp.sum(gh, axis=0, keepdims=True)
        sums_ref[2:3] = jnp.sum(gh * normed, axis=0, keepdims=True)
        sums_ref[3:8] = jnp.zeros((5, gh.shape[1]), f32)


def up_back(gz, w, middle, grad, branch, mods):
    slots, rows, c = gz.shape
    width = w.shape[1]
    block = lambda n: (n, 0, 0)
    whole = lambda n: (0, 0)
    return call(
        up_back_kernel,
        "up_back",
        (slots,),
        [
            (gz, (1, rows, c), block),
            (w, (1, width, c), block),
            (middle, None, None),
            (grad, None, None),
            (branch, None, None),
            (mods, None, None),
        ],
        [
            ((rows, width), f32, (rows, width), whole),
            ((rows, width), bf16, (rows, width), whole),
            ((8, width), f32, (8, width), whole),
        ],
        [pltpu.VMEM((rows, width), f32)],
        flops=2 * rows * width * c * slots,
    )


def out_back_kernel(where, one, two, w, ga, go_ref, keep_ref, away_ref, held):
    heads, tall, rows = one.shape
    count = heads * tall
    c = w.shape[2]
    i = where[0]
    chip, core = i // 2, lax.rem(i, 2)
    groups = keep_ref.shape[1]
    for half, some in enumerate((one, two)):
        flat = some[...].reshape(count, rows)
        found = jnp.zeros((count, rows), f32)
        for n in range(w.shape[0]):
            some_ga = ga[:, n * c : n * c + c]
            found = found + contract(w[n, half * count : half * count + count], some_ga, (1, 1))
            grad = contract(flat, some_ga, (1, 0)).astype(bf16)
            held[n, half * heads : half * heads + heads] = grad.reshape(heads, tall, c)
        go_ref[half * heads : half * heads + heads] = found.astype(bf16).reshape(heads, tall, rows)
    for slot in range(keep_ref.shape[0]):
        for group in range(groups):
            keep_ref[slot, group] = held[core, slot * groups + (chip ^ group)]
            away_ref[slot, group] = held[1 - core, slot * groups + (chip ^ group)]


def out_back(where, one, two, w, ga):
    heads, tall, rows = one.shape
    c = w.shape[2]
    shape = (heads // 2, 4, tall, c)
    zeros = lambda n: (0, 0, 0, 0)
    return call(
        out_back_kernel,
        "out_back",
        (1,),
        [
            (where, None, None),
            (one, None, None),
            (two, None, None),
            (w, None, None),
            (ga, None, None),
        ],
        [
            ((2 * heads, tall, rows), bf16, (2 * heads, tall, rows), lambda n: (0, 0, 0)),
            (shape, bf16, shape, zeros),
            (shape, bf16, shape, zeros),
        ],
        [pltpu.VMEM((2, 2 * heads, tall, c), bf16)],
    )


def weight_kernel(kinds, turned, *refs):
    left, left_far, right, right_far = refs[:4]
    outs = {}
    at = 4
    for kind in sorted(set(kinds)):
        outs[kind] = refs[at : at + 2]
        at += 2
    n = pl.program_id(0)

    def read(ref):
        return ref[0] if len(ref.shape) == 3 else ref[...]

    dims = (1, 1) if turned else (1, 0)
    found = contract(read(left), read(right), dims)
    found = (found + contract(read(left_far), read(right_far), dims)).astype(bf16)
    r = found.shape[0] // 4
    for kind, (send, keep) in outs.items():

        @pl.when((n >= kinds.index(kind)) & (n < kinds.index(kind) + kinds.count(kind)))
        def _():
            for m in range(2):
                for near, out in ((1, send), (0, keep)):
                    rel = (2 * near + m) if kind == 0 else (2 * m + near)
                    out[0, m] = found[rel * r : rel * r + r]


def weight_grads(left, left_far, right, right_far, kinds, turned=False):
    slots = len(kinds)
    r = left.shape[-2] // 4
    c = right.shape[-2] if turned else right.shape[-1]

    def spec(x):
        if len(x.shape) == 2:
            return (x, None, None)
        return (x, (1,) + x.shape[1:], lambda n: (n, 0, 0))

    outputs, order = [], sorted(set(kinds))
    for kind in order:
        low, count = kinds.index(kind), kinds.count(kind)
        index = lambda n, low=low, count=count: (jnp.clip(n - low, 0, count - 1), 0, 0, 0)
        outputs += [((count, 2, r, c), bf16, (1, 2, r, c), index)] * 2
    found = call(
        partial(weight_kernel, kinds, turned),
        "weight_grads",
        (slots,),
        [spec(left), spec(left_far), spec(right), spec(right_far)],
        outputs,
        flops=4 * slots * 4 * r * c * left.shape[-1],
    )
    return {kind: found[2 * n : 2 * n + 2] for n, kind in enumerate(order)}


def qkv_back_kernel(one, two, w, own_ref, other_ref, total):
    n = pl.program_id(0)
    half = pl.num_programs(0) // 2
    rows = own_ref.shape[0]

    @pl.when(n == 0)
    def _():
        total[...] = contract(w[0], one[0], (1, 0))

    @pl.when((n > 0) & (n < half))
    def _():
        total[...] += contract(w[0], one[0], (1, 0))

    @pl.when(n >= half)
    def _():
        total[...] += contract(w[0], two[0], (1, 0))

    @pl.when(n == pl.num_programs(0) - 1)
    def _():
        own_ref[...] = total[:, :rows].T
        other_ref[...] = total[:, rows:].T.astype(bf16)


def qkv_back(one, two, w):
    half, c, columns = one.shape
    slots, width, _ = w.shape
    rows = columns // 2
    return call(
        qkv_back_kernel,
        "qkv_back",
        (slots,),
        [
            (one, (1, c, columns), lambda n: (jnp.minimum(n, half - 1), 0, 0)),
            (two, (1, c, columns), lambda n: (jnp.maximum(n - half, 0), 0, 0)),
            (w, (1, width, c), lambda n: (n, 0, 0)),
        ],
        [
            ((rows, width), f32, (rows, width), lambda n: (0, 0)),
            ((rows, width), bf16, (rows, width), lambda n: (0, 0)),
        ],
        [pltpu.VMEM((width, columns), f32)],
        flops=2 * slots * c * columns * width,
    )


def last_kernel(own, far, tokens, gx, mods, out_ref, sums_ref):
    n = pl.program_id(0)
    gh = own[...] + far[...].astype(f32)
    normed, inverse = norm_parts(tokens[...].astype(f32))
    slope = gh * (1.0 + mods[1:2])
    mean_grad = jnp.mean(slope, axis=-1, keepdims=True)
    mean_inner = jnp.mean(slope * normed, axis=-1, keepdims=True)
    out_ref[...] = gx[...] + (slope - mean_grad - normed * mean_inner) * inverse

    @pl.when(n == 0)
    def _():
        sums_ref[...] = jnp.zeros(sums_ref.shape, f32)

    sums_ref[0:1] += jnp.sum(gh, axis=0, keepdims=True)
    sums_ref[1:2] += jnp.sum(gh * normed, axis=0, keepdims=True)


def last_part(own, far, tokens, gx, mods):
    rows, width = tokens.shape
    part = rows // 4
    row = lambda n: (n, 0)
    return call(
        last_kernel,
        "last",
        (4,),
        [
            (own, (part, width), row),
            (far, (part, width), row),
            (tokens, (part, width), row),
            (gx, (part, width), row),
            (mods, None, None),
        ],
        [
            ((rows, width), f32, (part, width), row),
            ((8, width), f32, (8, width), lambda n: (0, 0)),
        ],
    )


def land(halves, *earlier):
    landed = lax.optimization_barrier((*[half.flying for half in halves], *earlier))
    for half, got in zip(halves, landed):
        half.flying = got
    return [half.add() for half in halves]


class Relative:
    def __init__(self, parts, kind, bits):
        self.order = bits[::-1] if kind == 0 else list(bits)
        send, self.keep = parts
        self.send_part = send

    def send(self, *earlier):
        part = after(self.send_part, *earlier) if earlier else self.send_part
        self.flying = bit_swap(part, self.order[0])
        return self

    def add(self, *earlier):
        got = after(self.flying, *earlier) if earlier else self.flying
        self.order = self.order[1:]
        if self.order:
            self.send_part, self.keep = add(self.keep[:, 1], got[:, 1]), add(self.keep[:, 0], got[:, 0])
            return self.send_part
        self.keep = add(self.keep, got)
        return self.keep


def local_any(tokens, conditioning, master, moment, stats, roots, cotangent):
    dp_size = lax.axis_size("dp")
    tensor_size = lax.axis_size("tensor")
    i, t = lax.axis_index("dp"), lax.axis_index("tensor")
    where = jnp.stack([i, t]).astype(jnp.int32)
    rows, width = tokens.shape
    size = master.shape[1]
    sequences = conditioning.shape[0]
    latents = sequences * dp_size
    heads = HEADS // tensor_size
    shapes = grid_shapes(width, size, tensor_size)
    bits = [1 << b for b in range(1, dp_size.bit_length() - 1)]

    low = master.astype(bf16)
    pieces, spans, offset = [], [], 0
    for row_blocks, col_blocks in shapes:
        count = row_blocks * col_blocks // dp_size
        pieces.append(to_dense(low[offset : offset + count], col_blocks))
        spans.append((offset, offset + count))
        offset += count
    w_ada = pieces[4]

    head_cols = heads * HEAD_DIM
    ro, c_out = pieces[1].shape
    tall = HEAD_DIM + -HEAD_DIM % 16
    per = width // c_out
    pieces_out = jnp.pad(pieces[1], ((0, tall - ro), (0, 0)))
    one = Gathering(pieces[0], bits, relative=True)

    silu_low = jax.nn.silu(conditioning).astype(bf16)
    ada_cols = 6 * width // tensor_size
    ada_r, ada_c = w_ada.shape
    ada_per = ada_cols // ada_c
    row_at, col_at = (i // ada_per) * ada_r, (i % ada_per) * ada_c
    silu_for = jnp.moveaxis(silu_low.reshape(sequences, dp_size // ada_per, ada_r), 1, 0)
    silu_for = jnp.repeat(silu_for, ada_per, axis=0)
    silu_mine = exchange(silu_for, "dp").reshape(latents, ada_r)
    share = jnp.dot(silu_mine, w_ada, preferred_element_type=f32)
    if ada_per > 1:
        share = lax.dynamic_update_slice(jnp.zeros((latents, ada_cols), f32), share, (0, col_at))
    shares = exchange(share.reshape(dp_size, sequences, ada_cols), "dp")
    own_mods = jnp.sum(shares, axis=0)
    span = LEN // rows
    mods = exchange(jnp.repeat(own_mods, span, axis=0), "tensor").reshape(6, 1, width)
    shift1, scale1, gate1, shift2, scale2, gate2 = (mods[k] for k in range(6))

    two = WholeGathering(pieces_out, bits, *one.slots[1:])
    one.start()
    others = pair_swap(after(tokens, two.stack))
    three = Gathering(pieces[2], bits, two.stack)
    one.join(mods)
    one.last_send()
    one.cross()
    two.send(*one.flying)

    inputs = tokens.astype(f32)
    normed_one = layer_norm(inputs)
    h1 = (normed_one * (1.0 + scale1) + shift1).astype(bf16)
    h1_other = (layer_norm(others.astype(f32)) * (1.0 + scale1) + shift1).astype(bf16)
    h1_all = jnp.concatenate([h1, h1_other])
    two.join(h1_all)
    two.middle()
    two.send()
    w_qkv = whole_from_runs(one.assemble(dp_size, where, two.stack), width, 3 * head_cols)
    three.start()
    four = Gathering(pieces[3], bits, three.slots)
    h1_now = after(h1_all, *three.stacks)
    projected = jnp.einsum("tdc,rd->tcr", w_qkv, h1_now, preferred_element_type=f32).astype(bf16)
    projected = projected.reshape(tensor_size, 3 * heads, HEAD_DIM, 2 * rows)
    three.join(projected)
    three.last_send()
    two.join(projected)
    two.send()
    projected = after(projected, *three.stacks, two.stack)
    cut = tensor_size // 2
    first, first_log = attend(projected, heads, 0, cut)
    two.join(first)
    second, second_log = attend(
        after(projected, first, two.stack, *three.crossed), heads, cut, cut
    )
    attended = jnp.concatenate([first, second]).reshape(HEADS * tall, rows)
    out_parts = [(0, two.masks, after(two.stack, second, four.slots))]
    out_runs = assemble(out_parts, dp_size, where, relative=True)
    out_runs = out_runs.reshape(tensor_size, heads, per, tall, c_out)
    out_runs = jnp.moveaxis(out_runs, 2, 0).reshape(per, HEADS * tall, c_out)
    branch = jnp.concatenate(
        [
            jnp.einsum("er,ed->rd", attended, out_runs[n], preferred_element_type=f32)
            for n in range(per)
        ],
        axis=1,
    )
    middle = inputs + gate1 * branch
    normed_two = layer_norm(middle)
    h2 = (normed_two * (1.0 + scale2) + shift2).astype(bf16)
    three.cross(h2)
    four.start(*three.flying)
    w_up = whole_from_runs(three.assemble(dp_size, where, *four.stacks), width, FF // tensor_size)
    four.join(w_up)
    four.last_send()
    h2_now = after(h2, *four.stacks)
    pre_gelu = jnp.einsum("rd,tdc->trc", h2_now, w_up, preferred_element_type=f32)
    hidden = jax.nn.gelu(pre_gelu, approximate=True).astype(bf16)

    core = i % 2
    fast = all(pieces[n].shape[1] == shapes[n][1] * size for n in (0, 2, 3))
    lead = (2,) * len(bits)

    def core_part(values, axis, part):
        shape = values.shape
        shaped = values.reshape(shape[:axis] + (dp_size // 2, 2, shape[axis] // dp_size) + shape[axis + 1 :])
        taken = take(shaped, part, axis + 1)
        return taken.reshape(shape[:axis] + (shape[axis] // 2,) + shape[axis + 1 :])

    def both_cores(values, axis, columns=None, *earlier):
        keep = values if columns is None else core_part(values, columns, core)
        send = values if columns is None else core_part(values, columns, 1 - core)
        if earlier:
            send = after(send, *earlier)
        return jnp.concatenate([keep, bit_swap(send, 1)], axis=axis)

    def core_reduced(whole, shape):
        runs = runs_from_whole(whole, dp_size, *shape)
        runs = runs.reshape(runs.shape[:1] + (dp_size // 2, 2) + shape)
        got = bit_swap(take(runs, 1 - core, 2), 1)
        done = add(take(runs, core, 2), got)
        return done.reshape(runs.shape[:1] + lead + shape)

    def row_grads(spec, left, right, number):
        found = jnp.einsum(spec, left, right, preferred_element_type=f32).astype(bf16)
        if fast:
            return found.reshape(found.shape[:1] + lead + pieces[number].shape)
        return core_reduced(found, pieces[number].shape)

    def halves(runs):
        return [
            Reduction(runs[n * cut : n * cut + cut], bits, order, i)
            for n, order in enumerate((bits[::-1], bits))
        ]

    def send_all(*reductions, earlier=()):
        for half in reductions:
            if half.order:
                half.send(*earlier)

    grad_out = cotangent.astype(f32)
    gm = (grad_out * gate2).astype(bf16)
    if fast:
        hidden_all = both_cores(hidden, 1, 2)
        gm_all = both_cores(gm, 0, None, hidden)
    else:
        hidden_all, gm_all = hidden, gm
    four.cross(hidden_all)
    grad_down = row_grads("trc,rd->tcd", after(hidden_all, *four.flying, *four.crossed), gm_all, 3)
    red_down = halves(grad_down)
    send_all(*red_down)
    w_down = whole_from_runs(
        four.assemble(dp_size, where, grad_down), FF // tensor_size, width
    )
    gm_later = after(gm, grad_down)
    grad_hidden = jnp.einsum("rd,tcd->trc", gm_later, w_down, preferred_element_type=f32)
    _, gelu_pullback = jax.vjp(partial(jax.nn.gelu, approximate=True), pre_gelu)
    gz = gelu_pullback(grad_hidden)[0].astype(bf16)
    if fast:
        gz_all = both_cores(gz, 1)
        h2_all = both_cores(h2, 0, 1, gz)
    else:
        gz_all, h2_all = gz, h2
    gh2 = jnp.einsum("trc,tdc->rd", gz, w_up, preferred_element_type=f32)
    gx1 = grad_out + norm_back(middle, gh2 * (1.0 + scale2))
    ga = (gx1 * gate1).astype(bf16)
    down_two = [half.add(ga) for half in red_down]
    send_all(*red_down)
    ga = after(ga, *down_two)
    ga_runs = [ga[:, n * c_out : n * c_out + c_out] for n in range(per)]
    go = sum(
        jnp.einsum("ed,rd->er", out_runs[n], ga_runs[n], preferred_element_type=f32)
        for n in range(per)
    ).astype(bf16)
    go = go.reshape(HEADS, tall, rows)

    def out_grad(some):
        return jnp.einsum("er,rd->ed", attended, some, preferred_element_type=f32).astype(bf16)

    if fast:
        stacked = jnp.stack(ga_runs)
        keep, away = out_grad(take(stacked, core, 0)), out_grad(take(stacked, 1 - core, 0))
        grad_wo = add(keep, bit_swap(away, 1))
        grad_wo = grad_wo.reshape((tensor_size,) + lead + (tall, c_out))
    else:
        away = out_grad(ga)
        grad_wo = core_reduced(away.reshape(tensor_size, heads * tall, width), (tall, c_out))
    red_out = Reduction(grad_wo, bits, bits[::-1], i).send()
    grad_up = row_grads("rd,trc->tdc", h2_all, after(gz_all, grad_wo, go), 2)
    down_one = [half.last_add(grad_up) for half in red_down]
    down_spread = exchange_t(jnp.concatenate(down_one))
    red_up = halves(grad_up)
    send_all(*red_up, earlier=down_one)
    out_two = red_out.add(*down_one)
    send_all(red_out)
    first = attend_back(after(projected, out_two), go, first_log, heads, 0, cut)
    first = first.reshape(cut, 3 * head_cols, 2 * rows)
    out_one = red_out.last_add(first)
    first_all = both_cores(first, 2) if fast else first
    second = attend_back(after(projected, out_one), go, second_log, heads, cut, cut)
    second = second.reshape(cut, 3 * head_cols, 2 * rows)
    up_two = [half.add(second) for half in red_up]
    send_all(*red_up)
    second_all = both_cores(second, 2, None, first_all, *up_two) if fast else second
    state = (master, moment, stats, roots)
    done = step(after(down_spread, *up_two), spans[3], state, None)
    out_one = after(out_one[:, :ro], down_spread)
    out_slots = [take(out_one, (t + tensor_size - k) % tensor_size, 0) for k in range(tensor_size)]
    out_spread = exchange_t(jnp.stack(out_slots))
    h1_both = both_cores(h1_all, 0, 1, second) if fast else h1_all
    grad_first = row_grads("rd,tcr->tdc", h1_both, after(first_all, *done), 0)
    up_one = [half.last_add(grad_first) for half in red_up]
    red_first = Reduction(grad_first, bits, bits[::-1], i)
    red_first.send(*up_one)
    up_spread = exchange_t(after(jnp.concatenate(up_one), out_spread))
    gh1_other = jnp.einsum(
        "tcr,tdc->rd",
        after(jnp.concatenate([first, second]), *up_one, out_spread)[:, head_cols:, rows:],
        w_qkv[:, :, head_cols:],
        preferred_element_type=f32,
    ).astype(bf16)
    gh1_far = pair_swap(gh1_other)
    grad_second = row_grads("rd,tcr->tdc", h1_both, after(second_all, gh1_other), 0)
    red_second = Reduction(grad_second, bits, bits, i)
    red_second.send()
    done = step(after(out_spread, grad_second), spans[1], state, done)
    gh1 = jnp.einsum(
        "tcr,tdc->rd",
        after(jnp.concatenate([first, second])[:, :, :rows], *done),
        w_qkv,
        preferred_element_type=f32,
    )
    feed = jnp.einsum(
        "trc,tcd->rd", after(hidden, gh1), w_down, preferred_element_type=f32
    )
    result = (middle + gate2 * feed).astype(bf16)
    first_two = red_first.add(feed)
    second_two = red_second.add(feed)
    send_all(red_first, red_second)
    gh1 = after(gh1, *first_two, *second_two) + gh1_far.astype(f32)
    grad_tokens = gx1 + norm_back(inputs, gh1 * (1.0 + scale1))

    grad_mods = jnp.stack(
        [
            jnp.sum(gh1, axis=0),
            jnp.sum(gh1 * normed_one, axis=0),
            jnp.sum(gx1 * branch, axis=0),
            jnp.sum(gh2, axis=0),
            jnp.sum(gh2 * normed_two, axis=0),
            jnp.sum(grad_out * feed, axis=0),
        ]
    ).reshape(tensor_size, ada_cols)
    grad_mods = exchange_t(grad_mods)
    done = step(after(up_spread, grad_mods), spans[2], state, done)
    qkv_one = [red_first.last_add(*done), red_second.last_add(*done)]
    qkv_slots = [half[n] for half in qkv_one for n in range(cut)]
    qkv_spread = [qkv_slots[0]] + [
        shift_t(qkv_slots[k], tensor_size - k) for k in range(1, tensor_size)
    ]
    grad_mods = jnp.sum(grad_mods.reshape(sequences, span, ada_cols), axis=1)
    grad_mods = after(grad_mods, *qkv_one)
    if ada_per > 1:
        parts = jnp.moveaxis(grad_mods.reshape(sequences, ada_per, ada_c), 1, 0)
        grad_mods = jnp.tile(parts, (dp_size // ada_per, 1, 1))
    else:
        grad_mods = jnp.broadcast_to(grad_mods, (dp_size,) + grad_mods.shape)
    grad_mods = exchange(grad_mods, "dp").reshape(latents, ada_c)
    grad_ada = jnp.einsum("sr,sc->rc", silu_mine.astype(f32), grad_mods, precision=HIGHEST)
    grad_silu = jnp.einsum("sc,rc->sr", grad_mods, w_ada.astype(f32), precision=HIGHEST)
    grad_silu = exchange(grad_silu.reshape(dp_size, sequences, ada_r), "dp")
    grad_silu = jnp.sum(grad_silu.reshape(dp_size // ada_per, ada_per, sequences, ada_r), axis=1)
    grad_silu = jnp.moveaxis(grad_silu, 0, 1).reshape(sequences, width)
    done = step(after(grad_ada[None], grad_silu), spans[4], state, done)
    grad_silu = exchange_t(jnp.broadcast_to(grad_silu, (tensor_size,) + grad_silu.shape))
    grad_silu = jnp.sum(grad_silu, axis=0)
    _, silu_pullback = jax.vjp(jax.nn.silu, conditioning)
    grad_conditioning = silu_pullback(grad_silu)[0]
    done = step(after(jnp.stack(qkv_spread), *done), spans[0], state, done)
    return (result, grad_tokens, grad_conditioning, *done)


def local(tokens, conditioning, master, moment, stats, roots, cotangent):
    dp_size = lax.axis_size("dp")
    tensor_size = lax.axis_size("tensor")
    rows, width = tokens.shape
    size = master.shape[1]
    shapes = grid_shapes(width, size, tensor_size)
    counts = [row_blocks * col_blocks // dp_size for row_blocks, col_blocks in shapes]
    if dp_size != 8 or any(counts[n] % shapes[n][1] for n in (0, 2, 3, 4)):
        return local_any(tokens, conditioning, master, moment, stats, roots, cotangent)
    i, t = lax.axis_index("dp"), lax.axis_index("tensor")
    where = jnp.stack([i, t]).astype(jnp.int32)
    sequences = conditioning.shape[0]
    latents = sequences * dp_size
    heads = HEADS // tensor_size
    bits = [2, 4]
    low = master.astype(bf16)
    pieces, spans, offset = [], [], 0
    for count, (_, col_blocks) in zip(counts, shapes):
        pieces.append(to_dense(low[offset : offset + count], col_blocks))
        spans.append((offset, offset + count))
        offset += count
    w_ada = pieces[4]
    head_cols = heads * HEAD_DIM
    ro, c_out = pieces[1].shape
    tall = HEAD_DIM + -HEAD_DIM % 16
    per = width // c_out
    pieces_out = jnp.pad(pieces[1], ((0, tall - ro), (0, 0)))
    one = Gathering(pieces[0], bits, relative=True)

    silu_low = jax.nn.silu(conditioning).astype(bf16)
    ada_r, ada_c = w_ada.shape
    silu_for = jnp.moveaxis(silu_low.reshape(sequences, dp_size, ada_r), 1, 0)
    silu_mine = exchange(silu_for, "dp").reshape(latents, ada_r)
    share = jnp.dot(silu_mine, w_ada, preferred_element_type=f32)
    span = LEN // rows
    everyone = ("dp", "tensor")
    shares = exchange(jnp.repeat(share, span, axis=0), everyone)
    mods = jnp.sum(shares.reshape(dp_size, tensor_size, ada_c), axis=0).reshape(6, width)
    one.start()

    others = pair_swap(after(tokens, *one.slots[1:]))
    three = Gathering(pieces[2], bits, mods, *one.stacks)
    one.join()
    one.last_send()
    one.cross(mods)
    h1, h1_keep, h1_send = first(where, tokens, after(others, *one.flying), mods)
    two = WholeGathering(pieces_out, bits, three.slots)
    three.start(h1)
    w_qkv = whole_from_runs(
        one.assemble(dp_size, where, *three.stacks), width, 3 * head_cols
    )
    two.send(w_qkv)
    four = Gathering(pieces[3], bits, two.stack)
    h1_now = after(h1, two.stack).reshape(2 * rows, width)
    projected = jnp.einsum("tdc,rd->tcr", w_qkv, h1_now, preferred_element_type=f32).astype(bf16)
    projected = projected.reshape(tensor_size, 3 * heads, HEAD_DIM, 2 * rows)
    three.join(projected)
    three.last_send()
    two.join(projected)
    two.middle()
    two.send()
    projected = after(projected, *three.stacks, two.stack)
    cut = tensor_size // 2
    att_one, log_one = attend(projected, heads, 0, cut)
    two.join(att_one)
    two.send()
    att_two, log_two = attend(
        after(projected, att_one, two.stack, *three.crossed), heads, cut, cut
    )
    two.join(att_two)
    out_parts = [(0, two.masks, after(two.stack, four.slots))]
    w_out = assemble(out_parts, dp_size, where, relative=True, per=per)
    w_out = w_out.reshape(per, HEADS * tall, c_out)
    branch, middle, h2, h2_keep, h2_send = middle_part(
        where, att_one, att_two, w_out, tokens, mods
    )
    three.cross(h2)
    four.start(*three.flying)
    w_up = whole_from_runs(three.assemble(dp_size, where, *four.stacks), width, FF // tensor_size)
    four.join(w_up)
    four.last_send()
    hidden, slope, u_keep, u_send = up_part(where, after(h2, *four.stacks), w_up)

    gm = (cotangent.astype(f32) * mods[5]).astype(bf16)
    gm_far = bit_swap(after(gm, w_up), 1)
    four.cross(hidden)
    u_far = bit_swap(after(u_send, *four.flying), 1)
    grads = weight_grads(
        after(u_keep, *four.flying, *four.crossed), u_far, gm, gm_far, (0,) * cut + (1,) * cut
    )
    red_down = [Relative(grads[kind], kind, bits).send() for kind in range(2)]
    keeps = [half.keep for half in red_down]
    w_down = whole_from_runs(
        four.assemble(dp_size, where, *keeps), FF // tensor_size, width
    )
    gz = down_back(gm, w_down, slope)
    gx, ga, sums_two = up_back(gz, w_up, middle, cotangent, branch, mods)
    down_two = land(red_down, ga)
    for half in red_down:
        half.send()
    h2_far = bit_swap(after(h2_send, *down_two), 1)
    gz_far = bit_swap(after(gz, *down_two), 1)
    go, wo_keep, wo_away = out_back(where, att_one, att_two, w_out, after(ga, *down_two))
    wo_got = bit_swap(wo_away, 1)
    grads = weight_grads(
        h2_keep, h2_far, after(gz, go), gz_far, (0,) * cut + (1,) * cut
    )
    red_up = [Relative(grads[kind], kind, bits) for kind in range(2)]
    keeps = [half.keep for half in red_up]
    down_one = land(red_down, *keeps)
    down_spread = exchange_t(jnp.concatenate(down_one))
    for half in red_up:
        half.send(*down_one)
    wo_got = after(wo_got, *keeps)
    red_out = Relative((add(wo_keep[:, 2:], wo_got[:, 2:]), add(wo_keep[:, :2], wo_got[:, :2])), 0, bits)
    g_one = attend_back(after(projected, red_out.keep, *down_one), go, log_one, heads, 0, cut)
    g_one = g_one.reshape(cut, 3 * head_cols, 2 * rows)
    g_two = attend_back(after(projected, g_one), go, log_two, heads, cut, cut)
    g_two = g_two.reshape(cut, 3 * head_cols, 2 * rows)
    up_two = land(red_up, g_two, down_spread)
    for half in red_up:
        half.send()
    g_one_far = bit_swap(after(g_one, *up_two), 1)
    h1_far = bit_swap(after(h1_send, *up_two), 1)
    g_two_far = bit_swap(after(g_two, *up_two), 1)
    gh_own, gh_other = qkv_back(after(g_one, *up_two), g_two, w_qkv)
    up_one = land(red_up, gh_own)
    gh_far = pair_swap(after(gh_other, *up_one))
    up_spread = exchange_t(jnp.concatenate(up_one))
    grads = weight_grads(h1_keep, h1_far, after(g_one, *up_one), g_one_far, (0,) * cut, True)
    red_one = Relative(grads[0], 0, bits).send()
    red_out.send(red_one.keep)
    grads = weight_grads(
        h1_keep, h1_far, after(g_two, red_one.keep), g_two_far, (1,) * cut, True
    )
    red_two = Relative(grads[1], 1, bits).send()
    state = (master, moment, stats, roots)
    done = step(after(down_spread, red_two.keep), spans[3], state, None)
    result, sums_three = down_part(after(hidden, *done), w_down, middle, cotangent, mods)
    grad_tokens, sums_one = last_part(after(gh_own, result, up_spread), gh_far, tokens, gx, mods)
    one_two, two_two, out_two = land([red_one, red_two, red_out], grad_tokens)
    red_one.send()
    red_two.send()
    red_out.send()

    grad_mods = jnp.concatenate([sums_one[:2], sums_two[:3], sums_three[:1]])
    grad_mods = after(grad_mods.reshape(tensor_size, ada_c), one_two, two_two)
    grad_mods = jnp.broadcast_to(grad_mods, (dp_size,) + grad_mods.shape)
    grad_mods = exchange(grad_mods.reshape(-1, ada_c), everyone)
    grad_mods = jnp.sum(grad_mods.reshape(latents, span, ada_c), axis=1)
    grad_ada = jnp.einsum("sr,sc->rc", silu_mine.astype(f32), grad_mods, precision=HIGHEST)
    grad_silu = jnp.einsum("sc,rc->sr", grad_mods, w_ada.astype(f32), precision=HIGHEST)
    *qkv_one, out_one = land([red_one, red_two, red_out], grad_ada, grad_silu)
    qkv_slots = [half[n] for half in qkv_one for n in range(cut)]
    qkv_spread = [qkv_slots[0]] + [
        shift_t(qkv_slots[k], tensor_size - k) for k in range(1, tensor_size)
    ]
    grad_silu = after(grad_silu, *qkv_one).reshape(dp_size, 1, sequences, ada_r)
    grad_silu = jnp.broadcast_to(grad_silu, (dp_size, tensor_size, sequences, ada_r))
    grad_silu = exchange(grad_silu.reshape(-1, sequences, ada_r), everyone)
    done = step(after(up_spread, *qkv_one), spans[2], state, done)
    done = step(after(grad_ada[None], *done), spans[4], state, done)
    grad_silu = jnp.sum(grad_silu.reshape(dp_size, tensor_size, sequences, ada_r), axis=1)
    grad_silu = jnp.moveaxis(grad_silu, 0, 1).reshape(sequences, width)
    _, silu_pullback = jax.vjp(jax.nn.silu, conditioning)
    grad_conditioning = silu_pullback(grad_silu)[0]
    out_one = out_one[:, :ro]
    out_slots = [take(out_one, (t + tensor_size - k) % tensor_size, 0) for k in range(tensor_size)]
    out_spread = exchange_t(after(jnp.stack(out_slots), grad_silu))
    done = step(after(out_spread, *done), spans[1], state, done)
    done = step(after(jnp.stack(qkv_spread), *done), spans[0], state, done)
    return (result, grad_tokens, grad_conditioning, *done)


def solution(mesh):
    both = ("dp", "tensor")
    rows, blocks, pairs = P(both, None), P(both, None, None), P(None, both, None, None)
    return jax.shard_map(
        local,
        mesh=mesh,
        in_specs=(rows, P("dp", None), blocks, blocks, pairs, pairs, rows),
        out_specs=(rows, rows, P("dp", None), blocks, blocks, pairs),
        check_vma=False,
    )
```

```python
from functools import partial
import math

import jax
import jax.numpy as jnp
from jax import lax
from jax.experimental import pallas as pl
from jax.experimental.pallas import tpu as pltpu
from jax.sharding import PartitionSpec as P

HEADS = 16
HEAD_DIM = 72
FF = 4608
LEN = 1024

epsilon = 1e-06
momentum_decay = 0.9
learning_rate = 0.4
HIGHEST = lax.Precision.HIGHEST
bf16 = jnp.bfloat16
f32 = jnp.float32
VMEM_LIMIT = 56 * 1024 * 1024
SCALE = 0.001
TIMES = dict(
    first=6, middle=8, up=15, down=13, down_back=12, up_back=16, out_back=9, weight_grads=11, qkv_back=16, last=6
)


def cost(microseconds):
    return pl.CostEstimate(
        flops=int(SCALE * microseconds * 1.15e9), bytes_accessed=1024, transcendentals=0
    )


def layer_norm(values):
    center = values - jnp.mean(values, axis=-1, keepdims=True)
    variance = jnp.mean(center * center, axis=-1, keepdims=True)
    return center * lax.rsqrt(variance + epsilon)


def norm_back(values, gradient):
    center = values - jnp.mean(values, axis=-1, keepdims=True)
    variance = jnp.mean(center * center, axis=-1, keepdims=True)
    inverse = lax.rsqrt(variance + epsilon)
    normed = center * inverse
    mean_grad = jnp.mean(gradient, axis=-1, keepdims=True)
    mean_inner = jnp.mean(gradient * normed, axis=-1, keepdims=True)
    return (gradient - mean_grad - normed * mean_inner) * inverse


def grid_shapes(model_width, block_size, tensor_size):
    row_blocks = model_width // block_size
    split_size = block_size * tensor_size
    return [
        (row_blocks, 3 * model_width // split_size),
        (model_width // split_size, row_blocks),
        (row_blocks, FF // split_size),
        (FF // split_size, row_blocks),
        (row_blocks, 6 * model_width // split_size),
    ]


def to_dense(blocks, col_blocks):
    count, size = blocks.shape[0], blocks.shape[1]
    if count >= col_blocks:
        shaped = blocks.reshape(count // col_blocks, col_blocks, size, size)
        return jnp.transpose(shaped, (0, 2, 1, 3)).reshape(-1, col_blocks * size)
    return jnp.transpose(blocks, (1, 0, 2)).reshape(size, count * size)


def to_blocks(dense, size):
    rows, cols = dense.shape
    shaped = dense.reshape(rows // size, size, cols // size, size)
    return jnp.transpose(shaped, (0, 2, 1, 3)).reshape(-1, size, size)


def whole_from_runs(runs, rows, cols):
    tensor_size, dp_size, r, c = runs.shape
    per = cols // c
    if per == 1:
        return runs.reshape(tensor_size, rows, cols)
    shaped = runs.reshape(tensor_size, dp_size // per, per, r, c)
    return jnp.transpose(shaped, (0, 1, 3, 2, 4)).reshape(tensor_size, rows, cols)


def runs_from_whole(whole, dp_size, r, c):
    tensor_size, rows, cols = whole.shape
    per = cols // c
    if per == 1:
        return whole.reshape(tensor_size, dp_size, r, c)
    shaped = whole.reshape(tensor_size, dp_size // per, r, per, c)
    return jnp.transpose(shaped, (0, 1, 3, 2, 4)).reshape(tensor_size, dp_size, r, c)


def exchange(values, axis):
    return lax.all_to_all(values, axis, split_axis=0, concat_axis=0, tiled=True)


def bit_swap(values, bit):
    size = lax.axis_size("dp")
    return lax.ppermute(values, "dp", [(k, k ^ bit) for k in range(size)])


def ring(values):
    size = lax.axis_size("tensor")
    return lax.ppermute(values, "tensor", [(k, (k + 1) % size) for k in range(size)])


def pair_swap(values):
    size = lax.axis_size("tensor")
    return lax.ppermute(values, "tensor", [(k, k ^ 1) for k in range(size)])


def exchange_t(slots):
    return exchange(slots, "tensor")


def shift_t(values, k):
    size = lax.axis_size("tensor")
    return lax.ppermute(values, "tensor", [(n, (n + k) % size) for n in range(size)])


def after(values, *earlier):
    return lax.optimization_barrier((values, *earlier))[0]


class Gathering:
    def __init__(self, piece, bits, *earlier, relative=False):
        self.bits = bits
        size = lax.axis_size("tensor")
        piece = after(piece, *earlier) if earlier else piece
        if relative:
            self.slots = [piece] + [shift_t(piece, k) for k in range(1, size)]
        else:
            self.slots = exchange_t(jnp.broadcast_to(piece, (size,) + piece.shape))

    def start(self, *earlier):
        size = lax.axis_size("tensor")
        half = size // 2
        slots = self.slots
        if isinstance(slots, list):
            self.stacks = [jnp.stack(slots[n : n + half])[None] for n in (0, half)]
        else:
            self.stacks = [slots[None, :half], slots[None, half:]]
        if earlier:
            self.stacks = [after(stack, *earlier) for stack in self.stacks]
        self.masks = [[0], [0]]
        self.orders = [self.bits, self.bits[::-1]]
        return self.send()

    def send(self):
        self.flying = [bit_swap(stack, order[0]) for stack, order in zip(self.stacks, self.orders)]
        return self

    def join(self, *earlier):
        landed = lax.optimization_barrier((*self.flying, *earlier))
        for n, order in enumerate(self.orders):
            got = landed[n]
            self.masks[n] = self.masks[n] + [mask ^ order[0] for mask in self.masks[n]]
            self.stacks[n] = jnp.concatenate([self.stacks[n], got])
        self.orders = [order[1:] for order in self.orders]
        return self.stacks

    def last_send(self):
        while len(self.orders[0]) > 1:
            self.send()
            self.join()
        self.send()
        self.crossed = [bit_swap(stack, 1) for stack in self.stacks]
        return self

    def cross(self, *earlier):
        self.flying = list(lax.optimization_barrier((*self.flying, *earlier))[:2])
        self.last = [bit_swap(got, 1) for got in self.flying]
        return self.flying

    def parts(self):
        half = self.stacks[0].shape[1]
        found = []
        for n, order in enumerate(self.orders):
            near = self.masks[n]
            far = [mask ^ order[0] for mask in near]
            for masks, stack in (
                (near, self.stacks[n]),
                (far, self.flying[n]),
                ([mask ^ 1 for mask in near], self.crossed[n]),
                ([mask ^ 1 for mask in far], self.last[n]),
            ):
                found.append((n * half, masks, stack))
        return found

    def assemble(self, dp_size, where, *earlier):
        found = self.parts()
        if earlier:
            found[0] = found[0][:2] + (after(found[0][2], *earlier),)
        return assemble(found, dp_size, where)


class WholeGathering:
    def __init__(self, piece, bits, *earlier):
        size = lax.axis_size("tensor")
        piece = after(piece, *earlier)
        self.stack = exchange_t(jnp.broadcast_to(piece, (size,) + piece.shape))[None]
        self.masks, self.order = [0], list(bits) + [1]

    def send(self, *earlier):
        if earlier:
            self.stack = after(self.stack, *earlier)
        self.flying = bit_swap(self.stack, self.order[0])

    def join(self, *earlier):
        got = after(self.flying, *earlier) if earlier else self.flying
        self.stack = jnp.concatenate([self.stack, got])
        self.masks = self.masks + [mask ^ self.order[0] for mask in self.masks]
        self.order = self.order[1:]
        return self.stack

    def middle(self):
        while len(self.order) > 2:
            self.send()
            self.join()


def assemble_kernel(plan, relative, per, where, *refs):
    count = len(plan)
    stacks, out, held, sems = refs[:count], refs[count], refs[count + 1], refs[count + 2]
    i, t = where[0], where[1]
    size = out.shape[1 if per > 1 else 0]
    loads, stores = [], []
    for number, (first, masks) in enumerate(plan):
        slots = stacks[number].shape[1]
        for m, mask in enumerate(masks):
            for n in range(slots):
                slot = lax.rem(t + size - (first + n), size) if relative else first + n
                owner = i ^ mask
                place = (owner % per, slot, owner // per) if per > 1 else (slot, owner)
                sem = sems.at[len(loads)]
                loads.append(pltpu.make_async_copy(stacks[number].at[m, n], held.at[place], sem))
                stores.append(pltpu.make_async_copy(held.at[place], out.at[place], sem))
    for copy in loads:
        copy.start()
    for load, store in zip(loads, stores):
        load.wait()
        store.start()
    for copy in stores:
        copy.wait()


def assemble(found, dp_size, where, relative=False, per=1):
    plan = [(first, masks) for first, masks, _ in found]
    stacks = [stack for _, _, stack in found]
    r, c = stacks[0].shape[2:]
    slots = sum(stack.shape[1] * len(masks) for (_, masks), stack in zip(plan, stacks)) // dp_size
    shape = (per, slots, dp_size // per, r, c) if per > 1 else (slots, dp_size, r, c)
    amount = 2 * 2 * math.prod(shape)
    return pl.pallas_call(
        partial(assemble_kernel, plan, relative, per),
        out_shape=jax.ShapeDtypeStruct(shape, stacks[0].dtype),
        in_specs=[pl.BlockSpec(memory_space=pltpu.SMEM)]
        + [pl.BlockSpec(memory_space=pl.ANY)] * len(stacks),
        out_specs=pl.BlockSpec(memory_space=pl.ANY),
        scratch_shapes=[
            pltpu.VMEM(shape, stacks[0].dtype),
            pltpu.SemaphoreType.DMA((slots * dp_size,)),
        ],
        compiler_params=pltpu.CompilerParams(vmem_limit_bytes=VMEM_LIMIT),
        cost_estimate=cost(8.7),
        name="assemble",
    )(where, *stacks)


def take(values, index, axis):
    return lax.dynamic_index_in_dim(values, index, axis, keepdims=False)


def add(left, right):
    return (left.astype(f32) + right.astype(f32)).astype(bf16)


class Reduction:
    def __init__(self, runs, bits, order, i):
        self.left, self.order, self.i, self.runs = list(bits[::-1]), list(order), i, runs

    def send(self, *earlier):
        bit = self.order[0]
        other = take(self.runs, 1 - (self.i // bit) % 2, 1 + self.left.index(bit))
        self.flying = bit_swap(after(other, *earlier) if earlier else other, bit)
        return self

    def add(self, *earlier):
        bit = self.order.pop(0)
        got = after(self.flying, *earlier) if earlier else self.flying
        self.runs = add(take(self.runs, (self.i // bit) % 2, 1 + self.left.index(bit)), got)
        self.left.remove(bit)
        return self.runs

    def last_add(self, *earlier):
        self.add(*earlier)
        while self.order:
            self.send()
            self.add()
        return self.runs


def total(slots, *earlier):
    if earlier:
        slots = after(slots, *earlier)
    return jnp.sum(slots.astype(f32), axis=0)


def contract(left, right, dims):
    return lax.dot_general(left, right, ((dims[:1], dims[1:]), ((), ())), preferred_element_type=f32)


def attend_kernel(q_ref, k_ref, v_ref, k_other_ref, v_other_ref, out_ref, log_ref):
    factor = HEAD_DIM ** (-0.5) * math.log2(math.e)
    q = q_ref[0, 0]
    scores = [contract(keys[0, 0], q, (0, 0)) for keys in (k_ref, k_other_ref)]
    highest = jnp.max(scores[0], axis=0, keepdims=True)
    for piece in scores[1:]:
        highest = jnp.maximum(highest, jnp.max(piece, axis=0, keepdims=True))
    shift = highest * factor
    amount = jnp.zeros_like(shift)
    attended = jnp.zeros(q.shape, f32)
    for piece, values in zip(scores, (v_ref, v_other_ref)):
        weights = jnp.exp2(piece * factor - shift)
        amount = amount + jnp.sum(weights, axis=0, keepdims=True)
        attended = attended + contract(values[0, 0], weights.astype(bf16), (1, 0))
    size = q.shape[0]
    out_ref[0, :size] = (attended / amount).astype(bf16)
    out_ref[0, size:] = jnp.zeros((out_ref.shape[1] - size, q.shape[1]), bf16)
    log_ref[0] = shift + jnp.log2(amount)


def head_specs(heads, size, rows, start):
    def spec(part, column):
        return pl.BlockSpec(
            (1, 1, size, rows), lambda n: (start + n // heads, part * heads + n % heads, 0, column)
        )

    return [spec(0, 0), spec(1, 0), spec(2, 0), spec(1, 1), spec(2, 1)]


def attend(projected, heads, start, groups):
    _, _, size, columns = projected.shape
    rows = columns // 2
    count = groups * heads
    tall = size + -size % 16
    return pl.pallas_call(
        attend_kernel,
        grid=(count,),
        in_specs=head_specs(heads, size, rows, start),
        out_specs=[
            pl.BlockSpec((1, tall, rows), lambda n: (n, 0, 0)),
            pl.BlockSpec((1, 1, rows), lambda n: (n, 0, 0)),
        ],
        out_shape=[
            jax.ShapeDtypeStruct((count, tall, rows), bf16),
            jax.ShapeDtypeStruct((count, 1, rows), f32),
        ],
        compiler_params=pltpu.CompilerParams(vmem_limit_bytes=VMEM_LIMIT),
        cost_estimate=cost(10.6),
        name="attend",
    )(*[projected] * 5)


def attend_back_kernel(
    q_ref, k_ref, v_ref, k_other_ref, v_other_ref, grad_ref, log_ref, out_ref
):
    scale = HEAD_DIM ** (-0.5)
    factor = scale * math.log2(math.e)
    rows = q_ref.shape[3]
    q, log = q_ref[0, 0], log_ref[0]
    grad = grad_ref[0, : q.shape[0]]
    keys = [k_ref[0, 0], k_other_ref[0, 0]]
    values = [v_ref[0, 0], v_other_ref[0, 0]]
    weights = [jnp.exp2(contract(k, q, (0, 0)) * factor - log) for k in keys]
    grads = [contract(v, grad, (0, 0)) for v in values]
    inner = jnp.zeros_like(log)
    for w, g in zip(weights, grads):
        inner = inner + jnp.sum(w * g, axis=0, keepdims=True)
    grad_q = jnp.zeros(q.shape, f32)
    for place, (k, w, g) in enumerate(zip(keys, weights, grads)):
        columns = pl.ds(place * rows, rows)
        grad_v = contract(grad, w.astype(bf16), (1, 1))
        grad_scores = (w * (g - inner)).astype(bf16)
        grad_k = contract(q, grad_scores, (1, 1)) * scale
        grad_q = grad_q + contract(k, grad_scores, (1, 0))
        out_ref[0, 1, 0, :, columns] = grad_k.astype(bf16)
        out_ref[0, 2, 0, :, columns] = grad_v.astype(bf16)
    out_ref[0, 0, 0, :, pl.ds(0, rows)] = (grad_q * scale).astype(bf16)
    out_ref[0, 0, 0, :, pl.ds(rows, rows)] = jnp.zeros(q.shape, bf16)


def attend_back(projected, grad, log, heads, start, groups):
    _, _, size, columns = projected.shape
    rows = columns // 2
    count = groups * heads
    at = start * heads
    return pl.pallas_call(
        attend_back_kernel,
        grid=(count,),
        in_specs=head_specs(heads, size, rows, start)
        + [
            pl.BlockSpec((1, grad.shape[1], rows), lambda n: (at + n, 0, 0)),
            pl.BlockSpec((1, 1, rows), lambda n: (n, 0, 0)),
        ],
        out_specs=pl.BlockSpec(
            (1, 3, 1, size, columns), lambda n: (n // heads, 0, n % heads, 0, 0)
        ),
        out_shape=jax.ShapeDtypeStruct((groups, 3, heads, size, columns), bf16),
        compiler_params=pltpu.CompilerParams(vmem_limit_bytes=VMEM_LIMIT),
        cost_estimate=cost(16.6),
        name="attend_back",
    )(*[projected] * 5, grad, log)


def step_kernel(size, aliased, grads_ref, master_ref, moment_ref, stats_ref, roots_ref, *refs):
    new_master, new_moment, new_stats, held = refs[aliased:]
    n = pl.program_id(0)

    @pl.when(n == 0)
    def _():
        found = grads_ref[0].astype(f32)
        for k in range(1, grads_ref.shape[0]):
            found = found + grads_ref[k].astype(f32)
        held[...] = found

    rows = held[pl.ds(pl.multiple_of(n * size, 8), size), :]
    for b in range(master_ref.shape[0]):
        grad = rows[:, b * size : b * size + size]
        low = grad.astype(bf16)
        new_stats[0, b] = 0.5 * stats_ref[0, b] + 0.5 * contract(low, low, (1, 1))
        new_stats[1, b] = 0.5 * stats_ref[1, b] + 0.5 * contract(low, low, (0, 0))
        moment = momentum_decay * moment_ref[b] + (1.0 - momentum_decay) * grad
        new_moment[b] = moment
        update = contract(roots_ref[0, b].astype(bf16), moment.astype(bf16), (1, 0))
        update = contract(update.astype(bf16), roots_ref[1, b].astype(bf16), (1, 0))
        new_master[b] = master_ref[b] - learning_rate * update


def step(grads, span, state, earlier):
    master, moment, stats, roots = state
    size = master.shape[1]
    r, c = grads.shape[1:]
    steps, count = r // size, (span[1] - span[0]) // (r // size)
    base = span[0] // count
    blocks = pl.BlockSpec((count, size, size), lambda n: (base + n, 0, 0))
    pairs = pl.BlockSpec((2, count, size, size), lambda n: (0, base + n, 0, 0))
    aliased = list(earlier or ())
    amount = 40 * size * 128 * (span[1] - span[0])
    return pl.pallas_call(
        partial(step_kernel, size, len(aliased)),
        grid=(steps,),
        in_specs=[
            pl.BlockSpec(grads.shape, lambda n: (0, 0, 0)),
            blocks,
            blocks,
            pairs,
            pairs,
        ]
        + [pl.BlockSpec(memory_space=pl.ANY)] * len(aliased),
        out_specs=[blocks, blocks, pairs],
        out_shape=[jax.ShapeDtypeStruct(x.shape, f32) for x in (master, moment, stats)],
        scratch_shapes=[pltpu.VMEM((r, c), f32)],
        input_output_aliases={5 + n: n for n in range(len(aliased))},
        compiler_params=pltpu.CompilerParams(vmem_limit_bytes=VMEM_LIMIT),
        cost_estimate=cost(6.0),
        name="step",
    )(grads, master, moment, stats, roots, *aliased)


def call(kernel, name, grid, inputs, outputs, scratch=(), flops=0):
    amount = sum(math.prod(x.shape) * x.dtype.itemsize for x, _, _ in inputs)
    amount += sum(math.prod(shape) * jnp.dtype(kind).itemsize for shape, kind, _, _ in outputs)
    in_specs = []
    for x, block, index in inputs:
        if block is None and x.dtype == jnp.int32:
            in_specs.append(pl.BlockSpec(memory_space=pltpu.SMEM))
        elif block is None:
            in_specs.append(pl.BlockSpec(x.shape, lambda *_, rank=len(x.shape): (0,) * rank))
        else:
            in_specs.append(pl.BlockSpec(block, index))
    return pl.pallas_call(
        kernel,
        grid=grid,
        in_specs=in_specs,
        out_specs=[pl.BlockSpec(block, index) for _, _, block, index in outputs],
        out_shape=[jax.ShapeDtypeStruct(shape, kind) for shape, kind, _, _ in outputs],
        scratch_shapes=list(scratch),
        compiler_params=pltpu.CompilerParams(vmem_limit_bytes=VMEM_LIMIT),
        cost_estimate=cost(TIMES[name]),
        name=name,
    )(*[x for x, _, _ in inputs])


def split_rows(where, held, keep, send):
    rows = held.shape[0] // 8
    i = where[0]
    chip, core = i // 2, lax.rem(i, 2)
    for rel in range(4):
        for part, out in ((core, keep), (1 - core, send)):
            at = pl.multiple_of((2 * (chip ^ rel) + part) * rows, 16)
            out(rel * rows, held[pl.ds(at, rows), :])


def norm_parts(values):
    center = values - jnp.mean(values, axis=-1, keepdims=True)
    variance = jnp.mean(center * center, axis=-1, keepdims=True)
    inverse = lax.rsqrt(variance + epsilon)
    return center * inverse, inverse


def first_kernel(where, tokens, others, mods, h_ref, keep_ref, send_ref, held):
    rows = tokens.shape[0]
    for part, source in enumerate((tokens, others)):
        normed, _ = norm_parts(source[...].astype(f32))
        h = normed * (1.0 + mods[1:2]) + mods[0:1]
        h_ref[part] = h.astype(bf16)
        held[...] = h.T.astype(bf16)

        columns = pl.ds(part * rows, rows)

        def keep(at, values, columns=columns):
            keep_ref[pl.ds(at, values.shape[0]), columns] = values

        def send(at, values, columns=columns):
            send_ref[pl.ds(at, values.shape[0]), columns] = values

        split_rows(where, held, keep, send)


def first(where, tokens, others, mods):
    rows, width = tokens.shape
    half = (width // 2, 2 * rows)
    return call(
        first_kernel,
        "first",
        (1,),
        [(where, None, None), (tokens, None, None), (others, None, None), (mods, None, None)],
        [
            ((2, rows, width), bf16, (2, rows, width), lambda n: (0, 0, 0)),
            (half, bf16, half, lambda n: (0, 0)),
            (half, bf16, half, lambda n: (0, 0)),
        ],
        [pltpu.VMEM((width, rows), bf16)],
    )


def middle_kernel(
    where, one, two, w, tokens, mods, branch_ref, middle_ref, h_ref, keep_ref, send_ref, held
):
    count = one.shape[0] * one.shape[1]
    columns = one.shape[2]
    c = w.shape[2]
    for n in range(w.shape[0]):
        part = contract(one[...].reshape(count, columns), w[n, :count], (0, 0))
        part = part + contract(two[...].reshape(count, columns), w[n, count:], (0, 0))
        branch_ref[:, n * c : n * c + c] = part
    values = tokens[...].astype(f32) + mods[2:3] * branch_ref[...]
    middle_ref[...] = values
    normed, _ = norm_parts(values)
    h = normed * (1.0 + mods[4:5]) + mods[3:4]
    h_ref[...] = h.astype(bf16)
    held[...] = h.T.astype(bf16)

    def keep(at, values):
        keep_ref[pl.ds(at, values.shape[0]), :] = values

    def send(at, values):
        send_ref[pl.ds(at, values.shape[0]), :] = values

    split_rows(where, held, keep, send)


def middle_part(where, one, two, w, tokens, mods):
    rows, width = tokens.shape
    part = rows // 2
    heads, tall, _ = one.shape
    row = lambda n: (n, 0)
    column = lambda n: (0, n)
    return call(
        middle_kernel,
        "middle",
        (2,),
        [
            (where, None, None),
            (one, (heads, tall, part), lambda n: (0, 0, n)),
            (two, (heads, tall, part), lambda n: (0, 0, n)),
            (w, None, None),
            (tokens, (part, width), row),
            (mods, None, None),
        ],
        [
            ((rows, width), f32, (part, width), row),
            ((rows, width), f32, (part, width), row),
            ((rows, width), bf16, (part, width), row),
            ((width // 2, rows), bf16, (width // 2, part), column),
            ((width // 2, rows), bf16, (width // 2, part), column),
        ],
        [pltpu.VMEM((width, part), bf16)],
        flops=4 * rows * width * heads * tall,
    )


def up_kernel(where, h, w, u_ref, slope_ref, keep_ref, send_ref, held):
    root = math.sqrt(2.0 / math.pi)
    z = contract(h[...], w[0], (1, 0))
    square = z * z
    bent = jnp.tanh(root * z * (1.0 + 0.044715 * square))
    side = 0.5 * (1.0 + bent)
    u = z * side
    slope = side + 0.5 * z * (1.0 - bent * bent) * (root * (1.0 + 3 * 0.044715 * square))
    u_ref[0] = u.astype(bf16)
    slope_ref[0] = slope.astype(bf16)
    held[...] = u.T.astype(bf16)

    def keep(at, values):
        keep_ref[0, pl.ds(at, values.shape[0]), :] = values

    def send(at, values):
        send_ref[0, pl.ds(at, values.shape[0]), :] = values

    split_rows(where, held, keep, send)


def up_part(where, h, w):
    rows, width = h.shape
    slots, _, c = w.shape
    block = lambda n: (n, 0, 0)
    return call(
        up_kernel,
        "up",
        (slots,),
        [(where, None, None), (h, None, None), (w, (1, width, c), block)],
        [
            ((slots, rows, c), bf16, (1, rows, c), block),
            ((slots, rows, c), bf16, (1, rows, c), block),
            ((slots, c // 2, rows), bf16, (1, c // 2, rows), block),
            ((slots, c // 2, rows), bf16, (1, c // 2, rows), block),
        ],
        [pltpu.VMEM((c, rows), bf16)],
        flops=2 * rows * width * c * slots,
    )


def down_kernel(u, w, middle, grad, mods, out_ref, sums_ref, total):
    n = pl.program_id(0)
    part = contract(u[0], w[0], (1, 0))

    @pl.when(n == 0)
    def _():
        total[...] = part

    @pl.when(n > 0)
    def _():
        total[...] += part

    @pl.when(n == pl.num_programs(0) - 1)
    def _():
        feed = total[...]
        out_ref[...] = (middle[...] + mods[5:6] * feed).astype(bf16)
        sums_ref[...] = jnp.broadcast_to(
            jnp.sum(grad[...].astype(f32) * feed, axis=0, keepdims=True), sums_ref.shape
        )


def down_part(u, w, middle, grad, mods):
    slots, rows, c = u.shape
    width = w.shape[2]
    block = lambda n: (n, 0, 0)
    return call(
        down_kernel,
        "down",
        (slots,),
        [
            (u, (1, rows, c), block),
            (w, (1, c, width), block),
            (middle, None, None),
            (grad, None, None),
            (mods, None, None),
        ],
        [
            ((rows, width), bf16, (rows, width), lambda n: (0, 0)),
            ((8, width), f32, (8, width), lambda n: (0, 0)),
        ],
        [pltpu.VMEM((rows, width), f32)],
        flops=2 * rows * width * c * slots,
    )


def down_back_kernel(gm, w, slope, gz_ref):
    gz_ref[0] = (contract(gm[...], w[0], (1, 1)) * slope[0].astype(f32)).astype(bf16)


def down_back(gm, w, slope):
    slots, rows, c = slope.shape
    width = w.shape[2]
    block = lambda n: (n, 0, 0)
    return call(
        down_back_kernel,
        "down_back",
        (slots,),
        [(gm, None, None), (w, (1, c, width), block), (slope, (1, rows, c), block)],
        [((slots, rows, c), bf16, (1, rows, c), block)],
        flops=2 * rows * width * c * slots,
    )[0]


def up_back_kernel(gz, w, middle, grad, branch, mods, gx_ref, ga_ref, sums_ref, total):
    n = pl.program_id(0)
    part = contract(gz[0], w[0], (1, 1))

    @pl.when(n == 0)
    def _():
        total[...] = part

    @pl.when(n > 0)
    def _():
        total[...] += part

    @pl.when(n == pl.num_programs(0) - 1)
    def _():
        gh = total[...]
        normed, inverse = norm_parts(middle[...])
        slope = gh * (1.0 + mods[4:5])
        mean_grad = jnp.mean(slope, axis=-1, keepdims=True)
        mean_inner = jnp.mean(slope * normed, axis=-1, keepdims=True)
        gx = grad[...].astype(f32) + (slope - mean_grad - normed * mean_inner) * inverse
        gx_ref[...] = gx
        ga_ref[...] = (gx * mods[2:3]).astype(bf16)
        sums_ref[0:1] = jnp.sum(gx * branch[...], axis=0, keepdims=True)
        sums_ref[1:2] = jnp.sum(gh, axis=0, keepdims=True)
        sums_ref[2:3] = jnp.sum(gh * normed, axis=0, keepdims=True)
        sums_ref[3:8] = jnp.zeros((5, gh.shape[1]), f32)


def up_back(gz, w, middle, grad, branch, mods):
    slots, rows, c = gz.shape
    width = w.shape[1]
    block = lambda n: (n, 0, 0)
    whole = lambda n: (0, 0)
    return call(
        up_back_kernel,
        "up_back",
        (slots,),
        [
            (gz, (1, rows, c), block),
            (w, (1, width, c), block),
            (middle, None, None),
            (grad, None, None),
            (branch, None, None),
            (mods, None, None),
        ],
        [
            ((rows, width), f32, (rows, width), whole),
            ((rows, width), bf16, (rows, width), whole),
            ((8, width), f32, (8, width), whole),
        ],
        [pltpu.VMEM((rows, width), f32)],
        flops=2 * rows * width * c * slots,
    )


def out_back_kernel(where, one, two, w, ga, go_ref, keep_ref, away_ref, held):
    heads, tall, rows = one.shape
    count = heads * tall
    c = w.shape[2]
    i = where[0]
    chip, core = i // 2, lax.rem(i, 2)
    groups = keep_ref.shape[1]
    for half, some in enumerate((one, two)):
        flat = some[...].reshape(count, rows)
        found = jnp.zeros((count, rows), f32)
        for n in range(w.shape[0]):
            some_ga = ga[:, n * c : n * c + c]
            found = found + contract(w[n, half * count : half * count + count], some_ga, (1, 1))
            grad = contract(flat, some_ga, (1, 0)).astype(bf16)
            held[n, half * heads : half * heads + heads] = grad.reshape(heads, tall, c)
        go_ref[half * heads : half * heads + heads] = found.astype(bf16).reshape(heads, tall, rows)
    for slot in range(keep_ref.shape[0]):
        for group in range(groups):
            keep_ref[slot, group] = held[core, slot * groups + (chip ^ group)]
            away_ref[slot, group] = held[1 - core, slot * groups + (chip ^ group)]


def out_back(where, one, two, w, ga):
    heads, tall, rows = one.shape
    c = w.shape[2]
    shape = (heads // 2, 4, tall, c)
    zeros = lambda n: (0, 0, 0, 0)
    return call(
        out_back_kernel,
        "out_back",
        (1,),
        [
            (where, None, None),
            (one, None, None),
            (two, None, None),
            (w, None, None),
            (ga, None, None),
        ],
        [
            ((2 * heads, tall, rows), bf16, (2 * heads, tall, rows), lambda n: (0, 0, 0)),
            (shape, bf16, shape, zeros),
            (shape, bf16, shape, zeros),
        ],
        [pltpu.VMEM((2, 2 * heads, tall, c), bf16)],
    )


def weight_kernel(kinds, turned, *refs):
    left, left_far, right, right_far = refs[:4]
    outs = {}
    at = 4
    for kind in sorted(set(kinds)):
        outs[kind] = refs[at : at + 2]
        at += 2
    n = pl.program_id(0)

    def read(ref):
        return ref[0] if len(ref.shape) == 3 else ref[...]

    dims = (1, 1) if turned else (1, 0)
    found = contract(read(left), read(right), dims)
    found = (found + contract(read(left_far), read(right_far), dims)).astype(bf16)
    r = found.shape[0] // 4
    for kind, (send, keep) in outs.items():

        @pl.when((n >= kinds.index(kind)) & (n < kinds.index(kind) + kinds.count(kind)))
        def _():
            for m in range(2):
                for near, out in ((1, send), (0, keep)):
                    rel = (2 * near + m) if kind == 0 else (2 * m + near)
                    out[0, m] = found[rel * r : rel * r + r]


def weight_grads(left, left_far, right, right_far, kinds, turned=False):
    slots = len(kinds)
    r = left.shape[-2] // 4
    c = right.shape[-2] if turned else right.shape[-1]

    def spec(x):
        if len(x.shape) == 2:
            return (x, None, None)
        return (x, (1,) + x.shape[1:], lambda n: (n, 0, 0))

    outputs, order = [], sorted(set(kinds))
    for kind in order:
        low, count = kinds.index(kind), kinds.count(kind)
        index = lambda n, low=low, count=count: (jnp.clip(n - low, 0, count - 1), 0, 0, 0)
        outputs += [((count, 2, r, c), bf16, (1, 2, r, c), index)] * 2
    found = call(
        partial(weight_kernel, kinds, turned),
        "weight_grads",
        (slots,),
        [spec(left), spec(left_far), spec(right), spec(right_far)],
        outputs,
        flops=4 * slots * 4 * r * c * left.shape[-1],
    )
    return {kind: found[2 * n : 2 * n + 2] for n, kind in enumerate(order)}


def qkv_back_kernel(one, two, w, own_ref, other_ref, total):
    n = pl.program_id(0)
    half = pl.num_programs(0) // 2
    rows = own_ref.shape[0]

    @pl.when(n == 0)
    def _():
        total[...] = contract(w[0], one[0], (1, 0))

    @pl.when((n > 0) & (n < half))
    def _():
        total[...] += contract(w[0], one[0], (1, 0))

    @pl.when(n >= half)
    def _():
        total[...] += contract(w[0], two[0], (1, 0))

    @pl.when(n == pl.num_programs(0) - 1)
    def _():
        own_ref[...] = total[:, :rows].T
        other_ref[...] = total[:, rows:].T.astype(bf16)


def qkv_back(one, two, w):
    half, c, columns = one.shape
    slots, width, _ = w.shape
    rows = columns // 2
    return call(
        qkv_back_kernel,
        "qkv_back",
        (slots,),
        [
            (one, (1, c, columns), lambda n: (jnp.minimum(n, half - 1), 0, 0)),
            (two, (1, c, columns), lambda n: (jnp.maximum(n - half, 0), 0, 0)),
            (w, (1, width, c), lambda n: (n, 0, 0)),
        ],
        [
            ((rows, width), f32, (rows, width), lambda n: (0, 0)),
            ((rows, width), bf16, (rows, width), lambda n: (0, 0)),
        ],
        [pltpu.VMEM((width, columns), f32)],
        flops=2 * slots * c * columns * width,
    )


def last_kernel(own, far, tokens, gx, mods, out_ref, sums_ref):
    n = pl.program_id(0)
    gh = own[...] + far[...].astype(f32)
    normed, inverse = norm_parts(tokens[...].astype(f32))
    slope = gh * (1.0 + mods[1:2])
    mean_grad = jnp.mean(slope, axis=-1, keepdims=True)
    mean_inner = jnp.mean(slope * normed, axis=-1, keepdims=True)
    out_ref[...] = gx[...] + (slope - mean_grad - normed * mean_inner) * inverse

    @pl.when(n == 0)
    def _():
        sums_ref[...] = jnp.zeros(sums_ref.shape, f32)

    sums_ref[0:1] += jnp.sum(gh, axis=0, keepdims=True)
    sums_ref[1:2] += jnp.sum(gh * normed, axis=0, keepdims=True)


def last_part(own, far, tokens, gx, mods):
    rows, width = tokens.shape
    part = rows // 4
    row = lambda n: (n, 0)
    return call(
        last_kernel,
        "last",
        (4,),
        [
            (own, (part, width), row),
            (far, (part, width), row),
            (tokens, (part, width), row),
            (gx, (part, width), row),
            (mods, None, None),
        ],
        [
            ((rows, width), f32, (part, width), row),
            ((8, width), f32, (8, width), lambda n: (0, 0)),
        ],
    )


def land(halves, *earlier):
    landed = lax.optimization_barrier((*[half.flying for half in halves], *earlier))
    for half, got in zip(halves, landed):
        half.flying = got
    return [half.add() for half in halves]


class Relative:
    def __init__(self, parts, kind, bits):
        self.order = bits[::-1] if kind == 0 else list(bits)
        send, self.keep = parts
        self.send_part = send

    def send(self, *earlier):
        part = after(self.send_part, *earlier) if earlier else self.send_part
        self.flying = bit_swap(part, self.order[0])
        return self

    def add(self, *earlier):
        got = after(self.flying, *earlier) if earlier else self.flying
        self.order = self.order[1:]
        if self.order:
            self.send_part, self.keep = add(self.keep[:, 1], got[:, 1]), add(self.keep[:, 0], got[:, 0])
            return self.send_part
        self.keep = add(self.keep, got)
        return self.keep


def local_any(tokens, conditioning, master, moment, stats, roots, cotangent):
    dp_size = lax.axis_size("dp")
    tensor_size = lax.axis_size("tensor")
    i, t = lax.axis_index("dp"), lax.axis_index("tensor")
    where = jnp.stack([i, t]).astype(jnp.int32)
    rows, width = tokens.shape
    size = master.shape[1]
    sequences = conditioning.shape[0]
    latents = sequences * dp_size
    heads = HEADS // tensor_size
    shapes = grid_shapes(width, size, tensor_size)
    bits = [1 << b for b in range(1, dp_size.bit_length() - 1)]

    low = master.astype(bf16)
    pieces, spans, offset = [], [], 0
    for row_blocks, col_blocks in shapes:
        count = row_blocks * col_blocks // dp_size
        pieces.append(to_dense(low[offset : offset + count], col_blocks))
        spans.append((offset, offset + count))
        offset += count
    w_ada = pieces[4]

    head_cols = heads * HEAD_DIM
    ro, c_out = pieces[1].shape
    tall = HEAD_DIM + -HEAD_DIM % 16
    per = width // c_out
    pieces_out = jnp.pad(pieces[1], ((0, tall - ro), (0, 0)))
    one = Gathering(pieces[0], bits, relative=True)

    silu_low = jax.nn.silu(conditioning).astype(bf16)
    ada_cols = 6 * width // tensor_size
    ada_r, ada_c = w_ada.shape
    ada_per = ada_cols // ada_c
    row_at, col_at = (i // ada_per) * ada_r, (i % ada_per) * ada_c
    silu_for = jnp.moveaxis(silu_low.reshape(sequences, dp_size // ada_per, ada_r), 1, 0)
    silu_for = jnp.repeat(silu_for, ada_per, axis=0)
    silu_mine = exchange(silu_for, "dp").reshape(latents, ada_r)
    share = jnp.dot(silu_mine, w_ada, preferred_element_type=f32)
    if ada_per > 1:
        share = lax.dynamic_update_slice(jnp.zeros((latents, ada_cols), f32), share, (0, col_at))
    shares = exchange(share.reshape(dp_size, sequences, ada_cols), "dp")
    own_mods = jnp.sum(shares, axis=0)
    span = LEN // rows
    mods = exchange(jnp.repeat(own_mods, span, axis=0), "tensor").reshape(6, 1, width)
    shift1, scale1, gate1, shift2, scale2, gate2 = (mods[k] for k in range(6))

    two = WholeGathering(pieces_out, bits, *one.slots[1:])
    one.start()
    others = pair_swap(after(tokens, two.stack))
    three = Gathering(pieces[2], bits, two.stack)
    one.join(mods)
    one.last_send()
    one.cross()
    two.send(*one.flying)

    inputs = tokens.astype(f32)
    normed_one = layer_norm(inputs)
    h1 = (normed_one * (1.0 + scale1) + shift1).astype(bf16)
    h1_other = (layer_norm(others.astype(f32)) * (1.0 + scale1) + shift1).astype(bf16)
    h1_all = jnp.concatenate([h1, h1_other])
    two.join(h1_all)
    two.middle()
    two.send()
    w_qkv = whole_from_runs(one.assemble(dp_size, where, two.stack), width, 3 * head_cols)
    three.start()
    four = Gathering(pieces[3], bits, three.slots)
    h1_now = after(h1_all, *three.stacks)
    projected = jnp.einsum("tdc,rd->tcr", w_qkv, h1_now, preferred_element_type=f32).astype(bf16)
    projected = projected.reshape(tensor_size, 3 * heads, HEAD_DIM, 2 * rows)
    three.join(projected)
    three.last_send()
    two.join(projected)
    two.send()
    projected = after(projected, *three.stacks, two.stack)
    cut = tensor_size // 2
    first, first_log = attend(projected, heads, 0, cut)
    two.join(first)
    second, second_log = attend(
        after(projected, first, two.stack, *three.crossed), heads, cut, cut
    )
    attended = jnp.concatenate([first, second]).reshape(HEADS * tall, rows)
    out_parts = [(0, two.masks, after(two.stack, second, four.slots))]
    out_runs = assemble(out_parts, dp_size, where, relative=True)
    out_runs = out_runs.reshape(tensor_size, heads, per, tall, c_out)
    out_runs = jnp.moveaxis(out_runs, 2, 0).reshape(per, HEADS * tall, c_out)
    branch = jnp.concatenate(
        [
            jnp.einsum("er,ed->rd", attended, out_runs[n], preferred_element_type=f32)
            for n in range(per)
        ],
        axis=1,
    )
    middle = inputs + gate1 * branch
    normed_two = layer_norm(middle)
    h2 = (normed_two * (1.0 + scale2) + shift2).astype(bf16)
    three.cross(h2)
    four.start(*three.flying)
    w_up = whole_from_runs(three.assemble(dp_size, where, *four.stacks), width, FF // tensor_size)
    four.join(w_up)
    four.last_send()
    h2_now = after(h2, *four.stacks)
    pre_gelu = jnp.einsum("rd,tdc->trc", h2_now, w_up, preferred_element_type=f32)
    hidden = jax.nn.gelu(pre_gelu, approximate=True).astype(bf16)

    core = i % 2
    fast = all(pieces[n].shape[1] == shapes[n][1] * size for n in (0, 2, 3))
    lead = (2,) * len(bits)

    def core_part(values, axis, part):
        shape = values.shape
        shaped = values.reshape(shape[:axis] + (dp_size // 2, 2, shape[axis] // dp_size) + shape[axis + 1 :])
        taken = take(shaped, part, axis + 1)
        return taken.reshape(shape[:axis] + (shape[axis] // 2,) + shape[axis + 1 :])

    def both_cores(values, axis, columns=None, *earlier):
        keep = values if columns is None else core_part(values, columns, core)
        send = values if columns is None else core_part(values, columns, 1 - core)
        if earlier:
            send = after(send, *earlier)
        return jnp.concatenate([keep, bit_swap(send, 1)], axis=axis)

    def core_reduced(whole, shape):
        runs = runs_from_whole(whole, dp_size, *shape)
        runs = runs.reshape(runs.shape[:1] + (dp_size // 2, 2) + shape)
        got = bit_swap(take(runs, 1 - core, 2), 1)
        done = add(take(runs, core, 2), got)
        return done.reshape(runs.shape[:1] + lead + shape)

    def row_grads(spec, left, right, number):
        found = jnp.einsum(spec, left, right, preferred_element_type=f32).astype(bf16)
        if fast:
            return found.reshape(found.shape[:1] + lead + pieces[number].shape)
        return core_reduced(found, pieces[number].shape)

    def halves(runs):
        return [
            Reduction(runs[n * cut : n * cut + cut], bits, order, i)
            for n, order in enumerate((bits[::-1], bits))
        ]

    def send_all(*reductions, earlier=()):
        for half in reductions:
            if half.order:
                half.send(*earlier)

    grad_out = cotangent.astype(f32)
    gm = (grad_out * gate2).astype(bf16)
    if fast:
        hidden_all = both_cores(hidden, 1, 2)
        gm_all = both_cores(gm, 0, None, hidden)
    else:
        hidden_all, gm_all = hidden, gm
    four.cross(hidden_all)
    grad_down = row_grads("trc,rd->tcd", after(hidden_all, *four.flying, *four.crossed), gm_all, 3)
    red_down = halves(grad_down)
    send_all(*red_down)
    w_down = whole_from_runs(
        four.assemble(dp_size, where, grad_down), FF // tensor_size, width
    )
    gm_later = after(gm, grad_down)
    grad_hidden = jnp.einsum("rd,tcd->trc", gm_later, w_down, preferred_element_type=f32)
    _, gelu_pullback = jax.vjp(partial(jax.nn.gelu, approximate=True), pre_gelu)
    gz = gelu_pullback(grad_hidden)[0].astype(bf16)
    if fast:
        gz_all = both_cores(gz, 1)
        h2_all = both_cores(h2, 0, 1, gz)
    else:
        gz_all, h2_all = gz, h2
    gh2 = jnp.einsum("trc,tdc->rd", gz, w_up, preferred_element_type=f32)
    gx1 = grad_out + norm_back(middle, gh2 * (1.0 + scale2))
    ga = (gx1 * gate1).astype(bf16)
    down_two = [half.add(ga) for half in red_down]
    send_all(*red_down)
    ga = after(ga, *down_two)
    ga_runs = [ga[:, n * c_out : n * c_out + c_out] for n in range(per)]
    go = sum(
        jnp.einsum("ed,rd->er", out_runs[n], ga_runs[n], preferred_element_type=f32)
        for n in range(per)
    ).astype(bf16)
    go = go.reshape(HEADS, tall, rows)

    def out_grad(some):
        return jnp.einsum("er,rd->ed", attended, some, preferred_element_type=f32).astype(bf16)

    if fast:
        stacked = jnp.stack(ga_runs)
        keep, away = out_grad(take(stacked, core, 0)), out_grad(take(stacked, 1 - core, 0))
        grad_wo = add(keep, bit_swap(away, 1))
        grad_wo = grad_wo.reshape((tensor_size,) + lead + (tall, c_out))
    else:
        away = out_grad(ga)
        grad_wo = core_reduced(away.reshape(tensor_size, heads * tall, width), (tall, c_out))
    red_out = Reduction(grad_wo, bits, bits[::-1], i).send()
    grad_up = row_grads("rd,trc->tdc", h2_all, after(gz_all, grad_wo, go), 2)
    down_one = [half.last_add(grad_up) for half in red_down]
    down_spread = exchange_t(jnp.concatenate(down_one))
    red_up = halves(grad_up)
    send_all(*red_up, earlier=down_one)
    out_two = red_out.add(*down_one)
    send_all(red_out)
    first = attend_back(after(projected, out_two), go, first_log, heads, 0, cut)
    first = first.reshape(cut, 3 * head_cols, 2 * rows)
    out_one = red_out.last_add(first)
    first_all = both_cores(first, 2) if fast else first
    second = attend_back(after(projected, out_one), go, second_log, heads, cut, cut)
    second = second.reshape(cut, 3 * head_cols, 2 * rows)
    up_two = [half.add(second) for half in red_up]
    send_all(*red_up)
    second_all = both_cores(second, 2, None, first_all, *up_two) if fast else second
    state = (master, moment, stats, roots)
    done = step(after(down_spread, *up_two), spans[3], state, None)
    out_one = after(out_one[:, :ro], down_spread)
    out_slots = [take(out_one, (t + tensor_size - k) % tensor_size, 0) for k in range(tensor_size)]
    out_spread = exchange_t(jnp.stack(out_slots))
    h1_both = both_cores(h1_all, 0, 1, second) if fast else h1_all
    grad_first = row_grads("rd,tcr->tdc", h1_both, after(first_all, *done), 0)
    up_one = [half.last_add(grad_first) for half in red_up]
    red_first = Reduction(grad_first, bits, bits[::-1], i)
    red_first.send(*up_one)
    up_spread = exchange_t(after(jnp.concatenate(up_one), out_spread))
    gh1_other = jnp.einsum(
        "tcr,tdc->rd",
        after(jnp.concatenate([first, second]), *up_one, out_spread)[:, head_cols:, rows:],
        w_qkv[:, :, head_cols:],
        preferred_element_type=f32,
    ).astype(bf16)
    gh1_far = pair_swap(gh1_other)
    grad_second = row_grads("rd,tcr->tdc", h1_both, after(second_all, gh1_other), 0)
    red_second = Reduction(grad_second, bits, bits, i)
    red_second.send()
    done = step(after(out_spread, grad_second), spans[1], state, done)
    gh1 = jnp.einsum(
        "tcr,tdc->rd",
        after(jnp.concatenate([first, second])[:, :, :rows], *done),
        w_qkv,
        preferred_element_type=f32,
    )
    feed = jnp.einsum(
        "trc,tcd->rd", after(hidden, gh1), w_down, preferred_element_type=f32
    )
    result = (middle + gate2 * feed).astype(bf16)
    first_two = red_first.add(feed)
    second_two = red_second.add(feed)
    send_all(red_first, red_second)
    gh1 = after(gh1, *first_two, *second_two) + gh1_far.astype(f32)
    grad_tokens = gx1 + norm_back(inputs, gh1 * (1.0 + scale1))

    grad_mods = jnp.stack(
        [
            jnp.sum(gh1, axis=0),
            jnp.sum(gh1 * normed_one, axis=0),
            jnp.sum(gx1 * branch, axis=0),
            jnp.sum(gh2, axis=0),
            jnp.sum(gh2 * normed_two, axis=0),
            jnp.sum(grad_out * feed, axis=0),
        ]
    ).reshape(tensor_size, ada_cols)
    grad_mods = exchange_t(grad_mods)
    done = step(after(up_spread, grad_mods), spans[2], state, done)
    qkv_one = [red_first.last_add(*done), red_second.last_add(*done)]
    qkv_slots = [half[n] for half in qkv_one for n in range(cut)]
    qkv_spread = [qkv_slots[0]] + [
        shift_t(qkv_slots[k], tensor_size - k) for k in range(1, tensor_size)
    ]
    grad_mods = jnp.sum(grad_mods.reshape(sequences, span, ada_cols), axis=1)
    grad_mods = after(grad_mods, *qkv_one)
    if ada_per > 1:
        parts = jnp.moveaxis(grad_mods.reshape(sequences, ada_per, ada_c), 1, 0)
        grad_mods = jnp.tile(parts, (dp_size // ada_per, 1, 1))
    else:
        grad_mods = jnp.broadcast_to(grad_mods, (dp_size,) + grad_mods.shape)
    grad_mods = exchange(grad_mods, "dp").reshape(latents, ada_c)
    grad_ada = jnp.einsum("sr,sc->rc", silu_mine.astype(f32), grad_mods, precision=HIGHEST)
    grad_silu = jnp.einsum("sc,rc->sr", grad_mods, w_ada.astype(f32), precision=HIGHEST)
    grad_silu = exchange(grad_silu.reshape(dp_size, sequences, ada_r), "dp")
    grad_silu = jnp.sum(grad_silu.reshape(dp_size // ada_per, ada_per, sequences, ada_r), axis=1)
    grad_silu = jnp.moveaxis(grad_silu, 0, 1).reshape(sequences, width)
    done = step(after(grad_ada[None], grad_silu), spans[4], state, done)
    grad_silu = exchange_t(jnp.broadcast_to(grad_silu, (tensor_size,) + grad_silu.shape))
    grad_silu = jnp.sum(grad_silu, axis=0)
    _, silu_pullback = jax.vjp(jax.nn.silu, conditioning)
    grad_conditioning = silu_pullback(grad_silu)[0]
    done = step(after(jnp.stack(qkv_spread), *done), spans[0], state, done)
    return (result, grad_tokens, grad_conditioning, *done)


def local(tokens, conditioning, master, moment, stats, roots, cotangent):
    dp_size = lax.axis_size("dp")
    tensor_size = lax.axis_size("tensor")
    rows, width = tokens.shape
    size = master.shape[1]
    shapes = grid_shapes(width, size, tensor_size)
    counts = [row_blocks * col_blocks // dp_size for row_blocks, col_blocks in shapes]
    if dp_size != 8 or any(counts[n] % shapes[n][1] for n in (0, 2, 3, 4)):
        return local_any(tokens, conditioning, master, moment, stats, roots, cotangent)
    i, t = lax.axis_index("dp"), lax.axis_index("tensor")
    where = jnp.stack([i, t]).astype(jnp.int32)
    sequences = conditioning.shape[0]
    latents = sequences * dp_size
    heads = HEADS // tensor_size
    bits = [2, 4]
    low = master.astype(bf16)
    pieces, spans, offset = [], [], 0
    for count, (_, col_blocks) in zip(counts, shapes):
        pieces.append(to_dense(low[offset : offset + count], col_blocks))
        spans.append((offset, offset + count))
        offset += count
    w_ada = pieces[4]
    head_cols = heads * HEAD_DIM
    ro, c_out = pieces[1].shape
    tall = HEAD_DIM + -HEAD_DIM % 16
    per = width // c_out
    pieces_out = jnp.pad(pieces[1], ((0, tall - ro), (0, 0)))
    one = Gathering(pieces[0], bits, relative=True)

    silu_low = jax.nn.silu(conditioning).astype(bf16)
    ada_r, ada_c = w_ada.shape
    silu_for = jnp.moveaxis(silu_low.reshape(sequences, dp_size, ada_r), 1, 0)
    silu_mine = exchange(silu_for, "dp").reshape(latents, ada_r)
    share = jnp.dot(silu_mine, w_ada, preferred_element_type=f32)
    span = LEN // rows
    everyone = ("dp", "tensor")
    shares = exchange(jnp.repeat(share, span, axis=0), everyone)
    mods = jnp.sum(shares.reshape(dp_size, tensor_size, ada_c), axis=0).reshape(6, width)
    one.start()

    others = pair_swap(after(tokens, *one.slots[1:]))
    three = Gathering(pieces[2], bits, mods, *one.stacks)
    one.join()
    one.last_send()
    one.cross(mods)
    h1, h1_keep, h1_send = first(where, tokens, after(others, *one.flying), mods)
    two = WholeGathering(pieces_out, bits, three.slots)
    three.start(h1)
    w_qkv = whole_from_runs(
        one.assemble(dp_size, where, *three.stacks), width, 3 * head_cols
    )
    two.send(w_qkv)
    four = Gathering(pieces[3], bits, two.stack)
    h1_now = after(h1, two.stack).reshape(2 * rows, width)
    projected = jnp.einsum("tdc,rd->tcr", w_qkv, h1_now, preferred_element_type=f32).astype(bf16)
    projected = projected.reshape(tensor_size, 3 * heads, HEAD_DIM, 2 * rows)
    three.join(projected)
    three.last_send()
    two.join(projected)
    two.middle()
    two.send()
    projected = after(projected, *three.stacks, two.stack)
    cut = tensor_size // 2
    att_one, log_one = attend(projected, heads, 0, cut)
    two.join(att_one)
    two.send()
    att_two, log_two = attend(
        after(projected, att_one, two.stack, *three.crossed), heads, cut, cut
    )
    two.join(att_two)
    out_parts = [(0, two.masks, after(two.stack, four.slots))]
    w_out = assemble(out_parts, dp_size, where, relative=True, per=per)
    w_out = w_out.reshape(per, HEADS * tall, c_out)
    branch, middle, h2, h2_keep, h2_send = middle_part(
        where, att_one, att_two, w_out, tokens, mods
    )
    three.cross(h2)
    four.start(*three.flying)
    w_up = whole_from_runs(three.assemble(dp_size, where, *four.stacks), width, FF // tensor_size)
    four.join(w_up)
    four.last_send()
    hidden, slope, u_keep, u_send = up_part(where, after(h2, *four.stacks), w_up)

    gm = (cotangent.astype(f32) * mods[5]).astype(bf16)
    gm_far = bit_swap(after(gm, w_up), 1)
    four.cross(hidden)
    u_far = bit_swap(after(u_send, *four.flying), 1)
    grads = weight_grads(
        after(u_keep, *four.flying, *four.crossed), u_far, gm, gm_far, (0,) * cut + (1,) * cut
    )
    red_down = [Relative(grads[kind], kind, bits).send() for kind in range(2)]
    keeps = [half.keep for half in red_down]
    w_down = whole_from_runs(
        four.assemble(dp_size, where, *keeps), FF // tensor_size, width
    )
    gz = down_back(gm, w_down, slope)
    gx, ga, sums_two = up_back(gz, w_up, middle, cotangent, branch, mods)
    down_two = land(red_down, ga)
    for half in red_down:
        half.send()
    h2_far = bit_swap(after(h2_send, *down_two), 1)
    gz_far = bit_swap(after(gz, *down_two), 1)
    go, wo_keep, wo_away = out_back(where, att_one, att_two, w_out, after(ga, *down_two))
    wo_got = bit_swap(wo_away, 1)
    grads = weight_grads(
        h2_keep, h2_far, after(gz, go), gz_far, (0,) * cut + (1,) * cut
    )
    red_up = [Relative(grads[kind], kind, bits) for kind in range(2)]
    keeps = [half.keep for half in red_up]
    down_one = land(red_down, *keeps)
    down_spread = exchange_t(jnp.concatenate(down_one))
    wo_got = after(wo_got, *keeps)
    red_out = Relative((add(wo_keep[:, 2:], wo_got[:, 2:]), add(wo_keep[:, :2], wo_got[:, :2])), 0, bits)
    for half in red_up:
        half.send(*down_one)
    h1_far = bit_swap(after(h1_send, *down_one), 1)
    g_one = attend_back(after(projected, red_out.keep, *down_one), go, log_one, heads, 0, cut)
    g_one = g_one.reshape(cut, 3 * head_cols, 2 * rows)
    g_one_far = bit_swap(g_one, 1)
    g_two = attend_back(after(projected, g_one, h1_far), go, log_two, heads, cut, cut)
    g_two = g_two.reshape(cut, 3 * head_cols, 2 * rows)
    up_two = land(red_up, g_two, down_spread)
    for half in red_up:
        half.send()
    red_out.send(*up_two)
    g_two_far = bit_swap(after(g_two, *up_two), 1)
    gh_own, gh_other = qkv_back(after(g_one, *up_two), g_two, w_qkv)
    up_one = land(red_up, gh_own)
    gh_far = pair_swap(after(gh_other, *up_one))
    grads = weight_grads(h1_keep, h1_far, after(g_one, *up_one), g_one_far, (0,) * cut, True)
    red_one = Relative(grads[0], 0, bits).send()
    grads = weight_grads(
        h1_keep, h1_far, after(g_two, red_one.keep), g_two_far, (1,) * cut, True
    )
    red_two = Relative(grads[1], 1, bits).send()
    red_out.add(red_two.keep)
    red_out.send()
    grad_tokens, sums_one = last_part(after(gh_own, red_two.keep), gh_far, tokens, gx, mods)
    up_one = after(jnp.concatenate(up_one), gh_far)
    up_spread = [take(up_one, t, 0)] + [
        shift_t(take(up_one, (t + k) % tensor_size, 0), k) for k in range(1, tensor_size)
    ]
    result, sums_three = down_part(after(hidden, grad_tokens), w_down, middle, cotangent, mods)
    one_two, two_two, out_one = land([red_one, red_two, red_out], result)
    red_one.send()
    red_two.send()

    grad_mods = jnp.concatenate([sums_one[:2], sums_two[:3], sums_three[:1]])
    grad_mods = after(grad_mods.reshape(tensor_size, ada_c), one_two, two_two)
    grad_mods = jnp.broadcast_to(grad_mods, (dp_size,) + grad_mods.shape)
    grad_mods = exchange(grad_mods.reshape(-1, ada_c), everyone)
    grad_mods = jnp.sum(grad_mods.reshape(latents, span, ada_c), axis=1)
    grad_ada = jnp.einsum("sr,sc->rc", silu_mine.astype(f32), grad_mods, precision=HIGHEST)
    grad_silu = jnp.einsum("sc,rc->sr", grad_mods, w_ada.astype(f32), precision=HIGHEST)
    state = (master, moment, stats, roots)
    qkv_one = land([red_one, red_two], grad_ada, grad_silu)
    qkv_slots = [half[n] for half in qkv_one for n in range(cut)]
    qkv_spread = [qkv_slots[0]] + [
        shift_t(qkv_slots[k], tensor_size - k) for k in range(1, tensor_size)
    ]
    out_one = out_one[:, :ro]
    out_slots = [take(out_one, (t + tensor_size - k) % tensor_size, 0) for k in range(tensor_size)]
    out_spread = exchange_t(after(jnp.stack(out_slots), *qkv_one))
    done = step(after(down_spread, *qkv_one), spans[3], state, None)
    done = step(after(jnp.stack(up_spread), *qkv_one), spans[2], state, done)
    done = step(after(grad_ada[None], *done), spans[4], state, done)
    grad_silu = after(grad_silu, out_spread).reshape(dp_size, 1, sequences, ada_r)
    grad_silu = jnp.broadcast_to(grad_silu, (dp_size, tensor_size, sequences, ada_r))
    grad_silu = exchange(grad_silu.reshape(-1, sequences, ada_r), everyone)
    grad_silu = jnp.sum(grad_silu.reshape(dp_size, tensor_size, sequences, ada_r), axis=1)
    grad_silu = jnp.moveaxis(grad_silu, 0, 1).reshape(sequences, width)
    _, silu_pullback = jax.vjp(jax.nn.silu, conditioning)
    grad_conditioning = silu_pullback(grad_silu)[0]
    done = step(after(out_spread, *done), spans[1], state, done)
    done = step(after(jnp.stack(qkv_spread), *done), spans[0], state, done)
    return (result, grad_tokens, grad_conditioning, *done)


def solution(mesh):
    both = ("dp", "tensor")
    rows, blocks, pairs = P(both, None), P(both, None, None), P(None, both, None, None)
    return jax.shard_map(
        local,
        mesh=mesh,
        in_specs=(rows, P("dp", None), blocks, blocks, pairs, pairs, rows),
        out_specs=(rows, rows, P("dp", None), blocks, blocks, pairs),
        check_vma=False,
    )
```
